128 devices in a mesh: grp: 4 (over x), ep: 32 (over z, y, core).
Axes of the slice: x: 4, y: 4, z: 4, core: 2. Of those that a mesh axis runs over, the one named last changes fastest.
Arguments:
- base_tiles: bfloat16 [128, 3584, 1024], P(('grp', 'ep')), may hold values from -1.5 to 1.5
- adjusted_tiles: bfloat16 [256, 3584, 1024], P(('grp', 'ep')), may hold values from -1.5 to 1.5
- sketch: bfloat16 [1024, 128], replicated, may hold values from -6 to 6
- base_place: int32 [128], replicated, may hold values from 0 to 127, each once
- adjusted_place: int32 [128], replicated, may hold values from 0 to 255, as said below
- owner_map: int32 [128], replicated, may hold values from 0 to 127, each once
Outputs:
- scaled_basis: float32 [128, 3584, 128], P(('grp', 'ep'))
- projected: float32 [128, 128, 1024], P(('grp', 'ep'))
The draws below stay inside these ranges and needn't reach their ends.
Inputs may be any that keep to these rules, and one draw needn't show every extreme that they name: `base_place`: each slot once. `adjusted_place`: distinct slots; slot 2 d + s is slot s of device d; a quarter of the devices hold two adjusted windows, half hold one, a quarter none. `owner_map`: each device owns exactly one expert.
All inputs are finite; a program needn't handle non-finite values.
Results may differ from the reference program's by a relative error of at most 0.006.
Values may be sent and summed in bfloat16 or wider, within the bound.
A program may use at most 192 MiB of HBM per device.

```python
import math
import jax
import jax.numpy as jnp
from jax import lax

R = 3584
H = 1024
K = 128
POWER = 2
EXPERTS = 128


def draw_adjusted_place(key, part):
    key = jax.random.fold_in(key, 7)
    first_key, second_key = jax.random.split(key)
    ordering = jax.random.permutation(first_key, EXPERTS)
    middle = jax.random.permutation(second_key, EXPERTS - 2).astype(jnp.int32) + 1
    relabel = jnp.concatenate([jnp.array([0, EXPERTS - 1], jnp.int32), middle])
    steps = jnp.arange(EXPERTS, dtype=jnp.int32)
    halfway = EXPERTS // 2
    quarter = EXPERTS // 4
    device_pos = jnp.where(steps < halfway, steps // 2, steps - halfway + quarter)
    slot_pos = jnp.where(steps < halfway, steps % 2, 0)
    places = relabel[device_pos].astype(jnp.int32) * 2 + slot_pos
    return jnp.zeros((EXPERTS,), jnp.int32).at[ordering].set(places)


def level_of(rng, extent, shards, least, largest):
    def one(dim, shards_of):
        heights = jax.random.uniform(jax.random.fold_in(jax.random.fold_in(rng, 6), dim), (shards_of,), jnp.float32, least / len(shards), largest / len(shards))
        return jnp.repeat(jnp.exp(heights), extent[dim] // shards_of).reshape((-1,) + (1,) * (len(extent) - dim - 1))

    factor_of = one(*shards[0])
    for cut in shards[1:]:
        factor_of = factor_of * one(*cut)
    return factor_of


def normal_values(own_key, extent, width, most, cuts=(), held_as=jnp.bfloat16):
    drawn = jax.random.normal(own_key, extent, jnp.float32) * width
    if len(cuts) > 0:
        drawn = level_of(own_key, extent, cuts, -0.22, 0.18) * drawn
    return jnp.clip(drawn, min=-most, max=most).astype(held_as)


def setup_inputs(seed: int = 0) -> dict:
    key_list = jax.random.split(jax.random.key(seed), 7)
    return {
        "base_tiles": normal_values(key_list[0], (EXPERTS, R, H), 0.25, 1.5, ((0, 128),)),
        "adjusted_tiles": normal_values(key_list[1], (2 * EXPERTS, R, H), 0.25, 1.5, ((0, 128),)),
        "sketch": normal_values(key_list[2], (H, K), 1.0, 6.0),
        "base_place": jax.random.permutation(key_list[3], EXPERTS).astype(jnp.int32),
        "adjusted_place": draw_adjusted_place(jax.random.fold_in(key_list[6], 71), 0),
        "owner_map": jax.random.permutation(key_list[5], EXPERTS).astype(jnp.int32),
    }


highest = lax.Precision.HIGHEST

def orthonormal(columns):
    gram_matrix = lax.dot_general(columns.astype(jnp.float32), columns.astype(jnp.float32), (((0,), (0,)), ((), ())), precision=highest, preferred_element_type=jnp.float32)
    factor_low = jnp.linalg.cholesky(gram_matrix)
    return jax.scipy.linalg.solve_triangular(factor_low, columns.T, lower=True).T

def factorize(difference, sketch):
    current = orthonormal(jnp.dot(difference.astype(jnp.float32), sketch.astype(jnp.float32), preferred_element_type=jnp.float32))
    for repeat in range(POWER):
        rounded = current.astype(jnp.bfloat16)
        across = orthonormal(lax.dot_general(difference.astype(jnp.float32), rounded.astype(jnp.float32), (((0,), (0,)), ((), ())), preferred_element_type=jnp.float32))
        current = orthonormal(jnp.dot(difference.astype(jnp.float32), across.astype(jnp.bfloat16).astype(jnp.float32), preferred_element_type=jnp.float32))
    rounded = current.astype(jnp.bfloat16)
    projected = lax.dot_general(rounded.astype(jnp.float32), difference.astype(jnp.float32), (((0,), (0,)), ((), ())), preferred_element_type=jnp.float32)
    return (current * math.sqrt(R), projected)

def reference(base_tiles, adjusted_tiles, sketch, base_place, adjusted_place, owner_map):
    experts = jnp.arange(EXPERTS, dtype=jnp.int32)
    holder = jnp.zeros((EXPERTS,), jnp.int32).at[owner_map].set(experts)

    def single(position):
        expert = holder[position]
        adjusted_tile = lax.dynamic_index_in_dim(adjusted_tiles, adjusted_place[expert].astype(jnp.int32), 0, keepdims=False)
        base_tile = lax.dynamic_index_in_dim(base_tiles, base_place[expert].astype(jnp.int32), 0, keepdims=False)
        difference = (adjusted_tile.astype(jnp.float32) - base_tile.astype(jnp.float32)).astype(jnp.bfloat16)
        return factorize(difference, sketch)
    scaled_basis, projected = lax.map(single, experts)
    return (scaled_basis, projected)
```

```python
import functools
import math

import jax
import jax.numpy as jnp
from jax import lax
from jax.experimental import pallas as pl
from jax.experimental.pallas import tpu as pltpu
from jax.sharding import PartitionSpec as P

MESH = pl.DeviceIdType.MESH
N = 128
HI = lax.Precision.HIGHEST
F32=jnp.float32; BF=jnp.bfloat16
NT = (((1,),(1,)),((),()))
NN = (((1,),(0,)),((),()))
TN = (((0,),(0,)),((),()))
K=128; C=512; NC=7

def dot(a,b,dims,precision=None):
    return lax.dot_general(a,b,dims,precision=precision,preferred_element_type=F32)

def chol_inv(g_ref, m_ref, w_ref):
    sub = lax.broadcasted_iota(jnp.int32, (8,128), 0)
    a = g_ref[...]
    row = lax.broadcasted_iota(jnp.int32, (K,K), 0); col = lax.broadcasted_iota(jnp.int32, (K,K), 1)
    x = jnp.where(row==col, 1.0, 0.0).astype(F32)
    for j in range(16):
        r0 = 8*j
        p = a[:8]; xp = x[:8]
        s = {}
        for i in range(8):
            for k in range(i+1):
                s[i,k] = jnp.broadcast_to(p[i:i+1, r0+k:r0+k+1], (8,128))
        rows = [jnp.broadcast_to(p[i:i+1,:],(8,128)) for i in range(8)]
        xrows = [jnp.broadcast_to(xp[i:i+1,:],(8,128)) for i in range(8)]
        u = None; w = None
        for k in range(8):
            v = s[k,k]
            r = lax.rsqrt(v)
            uk = rows[k]*r; wk = xrows[k]*r
            u = uk if k==0 else jnp.where(sub==k, uk, u)
            w = wk if k==0 else jnp.where(sub==k, wk, w)
            l = {i: s[i,k]*r for i in range(k+1,8)}
            for i in range(k+1,8):
                for m in range(k+1,i+1):
                    s[i,m] = s[i,m]-l[i]*l[m]
            for i in range(k+1,8):
                rows[i] = rows[i]-l[i]*uk
                xrows[i] = xrows[i]-l[i]*wk
        w_ref[pl.ds(r0,8),:] = w
        if j<15:
            upd = dot(u, jnp.concatenate([u,w],axis=1), TN, HI)
            a = a[8:] - upd[r0+8:, :K]
            x = x[8:] - upd[r0+8:, K:]

def k2_kernel(adj_ref, base_ref, s_ref, out_ref, d, yt, zt, g, m, w, ab, bb, asem, bsem):
    def ca(c): return pltpu.make_async_copy(adj_ref.at[pl.ds(c*C,C)], ab.at[c], asem.at[c])
    def cb(c): return pltpu.make_async_copy(base_ref.at[pl.ds(c*C,C)], bb.at[c], bsem.at[c])
    for c in range(NC):
        ca(c).start(); cb(c).start()
    st = s_ref[...].astype(F32).T.astype(BF)
    g[...] = jnp.zeros_like(g)
    def first(c, car):
        ca(c).wait(); cb(c).wait()
        dc = (ab[c].astype(F32)-bb[c].astype(F32)).astype(BF)
        d[c] = dc
        y = dot(st, dc, NT)
        yt[c] = y
        g[...] += dot(y, y, NT, HI)
        return car
    lax.fori_loop(0,NC,first,0)
    def step(t, car):
        chol_inv(g, m, w)
        @pl.when(t%2==0)
        def _():
            zt[...] = jnp.zeros_like(zt)
            wv = w[...]
            def app(c, car):
                q = dot(wv, yt[c], NN, HI)
                qb = q.astype(BF)
                zt[...] += dot(qb, d[c], NN)
                @pl.when(t==4)
                def _():
                    out_ref[pl.ds(pl.multiple_of(c*C,C),C),:] = q.T.astype(BF)
                return car
            lax.fori_loop(0,NC,app,0)
            z = zt[...]
            g[...] = dot(z,z,NT,HI)
            @pl.when(t==4)
            def _():
                for j in range(8):
                    out_ref[3584+128*j:3584+128*(j+1),:] = zt[:,128*j:128*(j+1)].astype(BF)
        @pl.when(t%2==1)
        def _():
            at = dot(w[...], zt[...], NN, HI).astype(BF)
            g[...] = jnp.zeros_like(g)
            def back(c, car):
                y = dot(at, d[c], NT)
                yt[c] = y
                g[...] += dot(y,y,NT,HI)
                return car
            lax.fori_loop(0,NC,back,0)
        return car
    lax.fori_loop(0,5,step,0)

def k2(adj, base, sketch):
    return pl.pallas_call(k2_kernel,
        out_shape=jax.ShapeDtypeStruct((6144,128),BF),
        in_specs=[pl.BlockSpec(memory_space=pl.ANY)]*2+[pl.BlockSpec(memory_space=pltpu.VMEM)],
        out_specs=pl.BlockSpec(memory_space=pltpu.VMEM),
        scratch_shapes=[pltpu.VMEM((NC,C,1024),BF), pltpu.VMEM((NC,K,C),F32), pltpu.VMEM((K,1024),F32),
          pltpu.VMEM((K,K),F32), pltpu.VMEM((K,2*K),F32), pltpu.VMEM((K,K),F32),
          pltpu.VMEM((NC,C,1024),BF), pltpu.VMEM((NC,C,1024),BF), pltpu.SemaphoreType.DMA((NC,)), pltpu.SemaphoreType.DMA((NC,))],
        compiler_params=pltpu.CompilerParams(vmem_limit_bytes=48*2**20), name="factor")(adj,base,sketch)


def peer(o):
    x = lax.axis_index("grp")
    e = lax.axis_index("ep")
    o = (o * 37) % 128
    tx = (x + o // 32) % 4
    tz = (e // 8 + (o // 8) % 4) % 4
    ty = ((e // 2) % 4 + (o // 2) % 4) % 4
    tc = (e + o) % 2
    return tx, tz * 8 + ty * 2 + tc


def route_kernel(src_block, dst_block, slots, idx_ref, src_ref, dst_ref, got, out, ssem, rsem, s2sem, r2sem, lsem, l2sem):
    x = lax.axis_index("grp")
    e = lax.axis_index("ep")
    me = x * 32 + e
    mine = pl.ds(slots * me, slots)
    own = pltpu.make_async_copy(src_block(src_ref, me), got.at[mine], lsem)
    own.start()

    def spread(o, car):
        tx, te = peer(o)
        pltpu.make_async_remote_copy(
            src_block(src_ref, tx * 32 + te), got.at[mine], ssem, rsem, device_id=(tx, te), device_id_type=MESH
        ).start()
        return car

    lax.fori_loop(1, N, spread, 0)
    own.wait()
    most = got.at[pl.ds(0, slots * (N - 1))]
    pltpu.make_async_copy(most, most, rsem).wait()

    def pick(b, car):
        out[b] = got[idx_ref[b]]
        return car

    lax.fori_loop(0, N, pick, 0)
    own2 = pltpu.make_async_copy(out.at[me], dst_block(dst_ref, me), l2sem)
    own2.start()

    def collect(o, car):
        tx, te = peer(o)
        pltpu.make_async_remote_copy(
            out.at[tx * 32 + te], dst_block(dst_ref, me), s2sem, r2sem, device_id=(tx, te), device_id_type=MESH
        ).start()
        return car

    lax.fori_loop(1, N, collect, 0)
    pltpu.make_async_copy(most, most, ssem).wait()
    own2.wait()
    rest = out.at[pl.ds(0, N - 1)]
    pltpu.make_async_copy(rest, rest, r2sem).wait()
    pltpu.make_async_copy(rest, rest, s2sem).wait()


def route(src_block, dst_block, slots, piece, idx, src, shape, name):
    return pl.pallas_call(
        functools.partial(route_kernel, src_block, dst_block, slots),
        out_shape=jax.ShapeDtypeStruct(shape, BF),
        in_specs=[pl.BlockSpec(memory_space=pltpu.SMEM), pl.BlockSpec(memory_space=pl.ANY)],
        out_specs=pl.BlockSpec(memory_space=pl.ANY),
        scratch_shapes=[pltpu.VMEM((slots * N,) + piece, BF), pltpu.VMEM((N,) + piece, BF)]
        + [pltpu.SemaphoreType.DMA] * 6,
        compiler_params=pltpu.CompilerParams(has_side_effects=True, vmem_limit_bytes=48 * 2**20),
        name=name,
    )(idx, src)


def tile_rows(i):
    return pl.ds(pl.multiple_of((i // 4) * 112, 112), 112)


def tile_columns(i):
    return pl.ds(pl.multiple_of((i % 4) * 256, 256), 256)


def both_slots(ref, i):
    return ref.at[:, tile_rows(i), tile_columns(i)]


def one_tile(ref, i):
    return ref.at[tile_rows(i), tile_columns(i)]


def result_rows(ref, i):
    return ref.at[pl.ds(pl.multiple_of(i * 48, 48), 48)]


def result_rows_in(ref, i):
    return ref.at[pl.ds(0, 1), pl.ds(pl.multiple_of(i * 48, 48), 48)]


def by_key(key, value):
    places = lax.broadcasted_iota(jnp.int32, (N, N), 0)
    return jnp.sum(jnp.where(places == key[None, :], value[None, :], 0), axis=1, dtype=jnp.int32)


def shards(base_tiles, adjusted_tiles, sketch, base_place, adjusted_place, owner_map):
    adjusted_of = by_key(base_place, adjusted_place)
    result_of = by_key(owner_map, base_place)
    adjusted = route(both_slots, one_tile, 2, (112, 256), adjusted_of, adjusted_tiles, (3584, 1024), "move_adjusted")
    result = k2(adjusted, base_tiles[0], sketch)
    moved = route(result_rows_in, result_rows, 1, (48, 128), result_of, result[None], (6144, 128), "move_result")
    scaled_basis = moved[:3584].astype(F32) * math.sqrt(3584)
    projected = moved[3584:4608].astype(F32).reshape(8, 128, 128).transpose(1, 0, 2).reshape(128, 1024)
    return (scaled_basis[None], projected[None])


def solution(mesh):
    in_specs = (P(("grp", "ep"), None, None), P(("grp", "ep"), None, None), P(), P(), P(), P())
    out_specs = (P(("grp", "ep"), None, None), P(("grp", "ep"), None, None))
    return jax.shard_map(shards, mesh=mesh, in_specs=in_specs, out_specs=out_specs, check_vma=False)
```

```python
import functools
import math

import jax
import jax.numpy as jnp
from jax import lax
from jax.experimental import pallas as pl
from jax.experimental.pallas import tpu as pltpu
from jax.sharding import PartitionSpec as P

MESH = pl.DeviceIdType.MESH
N = 128
F32=jnp.float32; BF=jnp.bfloat16
NT = (((1,),(1,)),((),()))
NN = (((1,),(0,)),((),()))
TN = (((0,),(0,)),((),()))
K=128; C=512; NC=7

def dot(a,b,dims,precision=None):
    return lax.dot_general(a,b,dims,precision=precision,preferred_element_type=F32)

def split3(v):
    hi = v.astype(BF).astype(F32)
    rest = v - hi
    mid = rest.astype(BF).astype(F32)
    return hi, mid, rest - mid


def chol_inv(g_ref, w_ref):
    sub = lax.broadcasted_iota(jnp.int32, (8, K), 0)
    a = g_ref[...]
    row = lax.broadcasted_iota(jnp.int32, (K, K), 0)
    col = lax.broadcasted_iota(jnp.int32, (K, K), 1)
    x = jnp.where(row == col, 1.0, 0.0).astype(F32)
    for r0 in range(0, K, 8):
        p = a[:8]
        xp = x[:8]
        s = {}
        for i in range(8):
            for k in range(i + 1):
                s[i, k] = jnp.broadcast_to(p[i : i + 1, r0 + k : r0 + k + 1], (8, K))
        rows = [jnp.broadcast_to(p[i : i + 1, :], (8, K)) for i in range(8)]
        xrows = [jnp.broadcast_to(xp[i : i + 1, :], (8, K)) for i in range(8)]
        u = jnp.zeros((8, K), F32)
        w = jnp.zeros((8, K), F32)
        for k in range(8):
            r = lax.rsqrt(s[k, k])
            uk = rows[k] * r
            wk = xrows[k] * r
            u = jnp.where(sub == k, uk, u)
            w = jnp.where(sub == k, wk, w)
            l = {i: s[i, k] * r for i in range(k + 1, 8)}
            for i in range(k + 1, 8):
                for m in range(k + 1, i + 1):
                    s[i, m] = s[i, m] - l[i] * l[m]
            for i in range(k + 1, 8):
                rows[i] = rows[i] - l[i] * uk
                xrows[i] = xrows[i] - l[i] * wk
        w_ref[pl.ds(r0, 8), :] = w
        if r0 < K - 8:
            uh, um, ul = split3(u)
            wh, wm, wl = split3(w)
            left = jnp.concatenate([uh, uh, um, uh, ul, um], axis=0).astype(BF)
            right = jnp.concatenate(
                [
                    jnp.concatenate([uh, um, uh, ul, uh, um], axis=0).astype(BF),
                    jnp.concatenate([wh, wm, wh, wl, wh, wm], axis=0).astype(BF),
                ],
                axis=1,
            )
            upd = dot(left, right, TN)
            a = a[8:] - upd[r0 + 8 :, :K]
            x = x[8:] - upd[r0 + 8 :, K:]


def wide_left(v):
    hi = v.astype(BF)
    return jnp.concatenate([hi, hi, (v - hi.astype(F32)).astype(BF)], axis=1)


def wide_right(v):
    hi = v.astype(BF)
    return jnp.concatenate([hi, (v - hi.astype(F32)).astype(BF), hi], axis=0)


def gram(v):
    hi, mid, low = (part.astype(BF) for part in split3(v))
    first = dot(hi, jnp.concatenate([hi, mid, low], axis=0), NT)
    cross = first[:, K : 2 * K] + first[:, 2 * K :]
    return first[:, :K] + dot(mid, mid, NT) + cross + cross.T


def k2_kernel(adj_ref, base_ref, s_ref, out_ref, d, yt, zt, g, w, ab, bb, asem, bsem):
    def ca(c): return pltpu.make_async_copy(adj_ref.at[pl.ds(c*C,C)], ab.at[c], asem.at[c])
    def cb(c): return pltpu.make_async_copy(base_ref.at[pl.ds(c*C,C)], bb.at[c], bsem.at[c])
    for c in range(NC):
        ca(c).start(); cb(c).start()
    st = s_ref[...].astype(F32).T.astype(BF)
    g[...] = jnp.zeros_like(g)
    def first(c, car):
        ca(c).wait(); cb(c).wait()
        dc = (ab[c].astype(F32)-bb[c].astype(F32)).astype(BF)
        d[c] = dc
        y = dot(st, dc, NT)
        yt[c] = y
        g[...] += gram(y)
        return car
    lax.fori_loop(0,NC,first,0)
    def step(t, car):
        chol_inv(g, w)
        @pl.when(t%2==0)
        def _():
            zt[...] = jnp.zeros_like(zt)
            wv = wide_left(w[...])
            def app(c, car):
                q = dot(wv, wide_right(yt[c]), NN)
                qb = q.astype(BF)
                zt[...] += dot(qb, d[c], NN)
                @pl.when(t==4)
                def _():
                    out_ref[pl.ds(pl.multiple_of(c*C,C),C),:] = q.T.astype(BF)
                return car
            lax.fori_loop(0,NC,app,0)
            z = zt[...]
            g[...] = gram(z)
            @pl.when(t==4)
            def _():
                for j in range(8):
                    out_ref[3584+128*j:3584+128*(j+1),:] = zt[:,128*j:128*(j+1)].astype(BF)
        @pl.when(t%2==1)
        def _():
            at = dot(wide_left(w[...]), wide_right(zt[...]), NN).astype(BF)
            g[...] = jnp.zeros_like(g)
            def back(c, car):
                y = dot(at, d[c], NT)
                yt[c] = y
                g[...] += gram(y)
                return car
            lax.fori_loop(0,NC,back,0)
        return car
    lax.fori_loop(0,5,step,0)

def k2(adj, base, sketch):
    return pl.pallas_call(k2_kernel,
        out_shape=jax.ShapeDtypeStruct((6144,128),BF),
        in_specs=[pl.BlockSpec(memory_space=pl.ANY)]*2+[pl.BlockSpec(memory_space=pltpu.VMEM)],
        out_specs=pl.BlockSpec(memory_space=pltpu.VMEM),
        scratch_shapes=[pltpu.VMEM((NC,C,1024),BF), pltpu.VMEM((NC,K,C),F32), pltpu.VMEM((K,1024),F32),
          pltpu.VMEM((K,K),F32), pltpu.VMEM((K,K),F32),
          pltpu.VMEM((NC,C,1024),BF), pltpu.VMEM((NC,C,1024),BF), pltpu.SemaphoreType.DMA((NC,)), pltpu.SemaphoreType.DMA((NC,))],
        compiler_params=pltpu.CompilerParams(vmem_limit_bytes=48*2**20), name="factor")(adj,base,sketch)


def peer(o):
    x = lax.axis_index("grp")
    e = lax.axis_index("ep")
    o = (o * 101) % 128
    sign = 1 - 2 * (e % 2)
    tx = (x + 4 + sign * (o // 32)) % 4
    tz = (e // 8 + 4 + sign * ((o // 8) % 4)) % 4
    ty = ((e // 2) % 4 + 4 + sign * ((o // 2) % 4)) % 4
    return tx, tz * 8 + ty * 2 + (e + o) % 2


def route_kernel(src_block, dst_block, slots, chunks, idx_ref, src_ref, dst_ref, *scratch):
    parts = len(chunks)
    gots = scratch[:parts]
    outs = scratch[parts : 2 * parts]
    ssem, rsem, s2sem, r2sem, lsem, l2sem = scratch[2 * parts :]
    me = lax.axis_index("grp") * 32 + lax.axis_index("ep")
    mine = pl.ds(slots * me, slots)

    def own(k):
        return pltpu.make_async_copy(src_block(src_ref, me, *chunks[k]), gots[k].at[mine], lsem.at[k])

    def own2(k):
        return pltpu.make_async_copy(outs[k].at[me], dst_block(dst_ref, me, *chunks[k]), l2sem.at[k])

    for k in range(parts):
        own(k).start()

        def spread(o, car, k=k):
            tx, te = peer(o)
            pltpu.make_async_remote_copy(
                src_block(src_ref, tx * 32 + te, *chunks[k]),
                gots[k].at[mine],
                ssem.at[k],
                rsem.at[k],
                device_id=(tx, te),
                device_id_type=MESH,
            ).start()
            return car

        lax.fori_loop(1, N, spread, 0)
    for k in range(parts):
        own(k).wait()
        most = gots[k].at[pl.ds(0, slots * (N - 1))]
        pltpu.make_async_copy(most, most, rsem.at[k]).wait()

        def pick(b, car, k=k):
            outs[k][b] = gots[k][idx_ref[b]]
            return car

        lax.fori_loop(0, N, pick, 0)
        own2(k).start()

        def collect(o, car, k=k):
            tx, te = peer(o)
            pltpu.make_async_remote_copy(
                outs[k].at[tx * 32 + te],
                dst_block(dst_ref, me, *chunks[k]),
                s2sem.at[k],
                r2sem.at[k],
                device_id=(tx, te),
                device_id_type=MESH,
            ).start()
            return car

        lax.fori_loop(1, N, collect, 0)
    for k in range(parts):
        own2(k).wait()
        most = gots[k].at[pl.ds(0, slots * (N - 1))]
        pltpu.make_async_copy(most, most, ssem.at[k]).wait()
        rest = outs[k].at[pl.ds(0, N - 1)]
        pltpu.make_async_copy(rest, rest, r2sem.at[k]).wait()
        pltpu.make_async_copy(rest, rest, s2sem.at[k]).wait()


def route(src_block, dst_block, slots, columns, chunks, idx, src, shape, name):
    return pl.pallas_call(
        functools.partial(route_kernel, src_block, dst_block, slots, chunks),
        out_shape=jax.ShapeDtypeStruct(shape, BF),
        in_specs=[pl.BlockSpec(memory_space=pltpu.SMEM), pl.BlockSpec(memory_space=pl.ANY)],
        out_specs=pl.BlockSpec(memory_space=pl.ANY),
        scratch_shapes=[pltpu.VMEM((slots * N, rows, columns), BF) for _, rows in chunks]
        + [pltpu.VMEM((N, rows, columns), BF) for _, rows in chunks]
        + [pltpu.SemaphoreType.DMA((len(chunks),))] * 6,
        compiler_params=pltpu.CompilerParams(has_side_effects=True, vmem_limit_bytes=48 * 2**20),
        name=name,
    )(idx, src)


def tile(i, first, rows):
    return pl.ds(pl.multiple_of((i // 4) * 112 + first, 16), rows), pl.ds(pl.multiple_of((i % 4) * 256, 256), 256)


def both_slots(ref, i, first, rows):
    high, wide = tile(i, first, rows)
    return ref.at[:, high, wide]


def one_tile(ref, i, first, rows):
    high, wide = tile(i, first, rows)
    return ref.at[high, wide]


def result_rows(ref, i, first, rows):
    return ref.at[pl.ds(pl.multiple_of(i * 48 + first, 16), rows)]


def result_rows_in(ref, i, first, rows):
    return ref.at[pl.ds(0, 1), pl.ds(pl.multiple_of(i * 48 + first, 16), rows)]


def by_key(key, value):
    places = lax.broadcasted_iota(jnp.int32, (N, N), 0)
    return jnp.sum(jnp.where(places == key[None, :], value[None, :], 0), axis=1, dtype=jnp.int32)


def shards(base_tiles, adjusted_tiles, sketch, base_place, adjusted_place, owner_map):
    adjusted_of = by_key(base_place, adjusted_place)
    result_of = by_key(owner_map, base_place)
    chunks = ((0, 32), (32, 32), (64, 32), (96, 16))
    adjusted = route(both_slots, one_tile, 2, 256, chunks, adjusted_of, adjusted_tiles, (3584, 1024), "move_adjusted")
    result = k2(adjusted, base_tiles[0], sketch)
    moved = route(result_rows_in, result_rows, 1, 128, ((0, 48),), result_of, result[None], (6144, 128), "move_result")
    scaled_basis = moved[:3584].astype(F32) * math.sqrt(3584)
    projected = moved[3584:4608].astype(F32).reshape(8, 128, 128).transpose(1, 0, 2).reshape(128, 1024)
    return (scaled_basis[None], projected[None])


def solution(mesh):
    in_specs = (P(("grp", "ep"), None, None), P(("grp", "ep"), None, None), P(), P(), P(), P())
    out_specs = (P(("grp", "ep"), None, None), P(("grp", "ep"), None, None))
    return jax.shard_map(shards, mesh=mesh, in_specs=in_specs, out_specs=out_specs, check_vma=False)
```

```python
import math

import jax
import jax.numpy as jnp
from jax import lax
from jax.experimental import pallas as pl
from jax.experimental.pallas import tpu as pltpu
from jax.sharding import PartitionSpec as P

MESH = pl.DeviceIdType.MESH
N = 128
CHUNKS = ((0, 32), (32, 32), (64, 32), (96, 16))
F32 = jnp.float32
BF = jnp.bfloat16
NT = (((1,), (1,)), ((), ()))
NN = (((1,), (0,)), ((), ()))
TN = (((0,), (0,)), ((), ()))
K = 128
C = 512
NC = 7

def dot(a, b, dims):
    return lax.dot_general(a, b, dims, preferred_element_type=F32)

def split3(v):
    hi = v.astype(BF).astype(F32)
    rest = v - hi
    mid = rest.astype(BF).astype(F32)
    return hi, mid, rest - mid


def chol_inv(g_ref, w_ref):
    sub = lax.broadcasted_iota(jnp.int32, (8, K), 0)
    a = g_ref[...]
    row = lax.broadcasted_iota(jnp.int32, (K, K), 0)
    col = lax.broadcasted_iota(jnp.int32, (K, K), 1)
    x = jnp.where(row == col, 1.0, 0.0).astype(F32)
    for r0 in range(0, K, 8):
        p = a[:8]
        xp = x[:8]
        s = {}
        for i in range(8):
            for k in range(i + 1):
                s[i, k] = jnp.broadcast_to(p[i : i + 1, r0 + k : r0 + k + 1], (8, K))
        rows = [jnp.broadcast_to(p[i : i + 1, :], (8, K)) for i in range(8)]
        xrows = [jnp.broadcast_to(xp[i : i + 1, :], (8, K)) for i in range(8)]
        u = jnp.zeros((8, K), F32)
        w = jnp.zeros((8, K), F32)
        for k in range(8):
            r = lax.rsqrt(s[k, k])
            uk = rows[k] * r
            wk = xrows[k] * r
            u = jnp.where(sub == k, uk, u)
            w = jnp.where(sub == k, wk, w)
            l = {i: s[i, k] * r for i in range(k + 1, 8)}
            for i in range(k + 1, 8):
                for m in range(k + 1, i + 1):
                    s[i, m] = s[i, m] - l[i] * l[m]
            for i in range(k + 1, 8):
                rows[i] = rows[i] - l[i] * uk
                xrows[i] = xrows[i] - l[i] * wk
        w_ref[pl.ds(r0, 8), :] = w
        if r0 < K - 8:
            uh, um, ul = split3(u)
            wh, wm, wl = split3(w)
            left = jnp.concatenate([uh, uh, um, uh, ul, um], axis=0).astype(BF)
            right = jnp.concatenate(
                [
                    jnp.concatenate([uh, um, uh, ul, uh, um], axis=0).astype(BF),
                    jnp.concatenate([wh, wm, wh, wl, wh, wm], axis=0).astype(BF),
                ],
                axis=1,
            )
            upd = dot(left, right, TN)
            a = a[8:] - upd[r0 + 8 :, :K]
            x = x[8:] - upd[r0 + 8 :, K:]


def wide_left(v):
    hi = v.astype(BF)
    return jnp.concatenate([hi, hi, (v - hi.astype(F32)).astype(BF)], axis=1)


def wide_right(v):
    hi = v.astype(BF)
    return jnp.concatenate([hi, (v - hi.astype(F32)).astype(BF), hi], axis=0)


def gram(v):
    hi, mid, low = (part.astype(BF) for part in split3(v))
    first = dot(hi, jnp.concatenate([hi, mid, low], axis=0), NT)
    cross = first[:, K : 2 * K] + first[:, 2 * K :]
    return first[:, :K] + dot(mid, mid, NT) + cross + cross.T


def peer(o):
    x = lax.axis_index("grp")
    e = lax.axis_index("ep")
    o = (o * 101) % 128
    sign = 1 - 2 * (e % 2)
    tx = (x + 4 + sign * (o // 32)) % 4
    tz = (e // 8 + 4 + sign * ((o // 8) % 4)) % 4
    ty = ((e // 2) % 4 + 4 + sign * ((o // 2) % 4)) % 4
    return tx, tz * 8 + ty * 2 + (e + o) % 2


def whole(device):
    return None


def push(src, dst, send_sem, recv_sem, when=whole):
    def one(o, car):
        tx, te = peer(o)
        t = tx * 32 + te

        def start():
            pltpu.make_async_remote_copy(
                src(t), dst(t), send_sem, recv_sem, device_id=(tx, te), device_id_type=MESH
            ).start()

        if when is whole:
            start()
        else:
            pl.when(when(t))(start)
        return car

    lax.fori_loop(1, N, one, 0)


def wait_for(ref, count, sem):
    part = ref.at[pl.ds(0, count)]
    pltpu.make_async_copy(part, part, sem).wait()


def tile(i, chunk):
    first, rows = chunk
    return i // 4, pl.ds(first, rows), pl.ds(pl.multiple_of((i % 4) * 256, 256), 256)


def basis_rows(ref, i):
    return ref.at[pl.ds((i // 7) * 2, 2), pl.ds(pl.multiple_of((i % 7) * 16, 16), 16)]


def projected_rows(ref, i):
    return ref.at[pl.ds(pl.multiple_of((i // 2) * 16, 16), 16)]


def kernel(adjusted_of, result_of, adjusted, base, sketch, basis_out, projected_out, *scratch):
    parts = len(CHUNKS)
    gots = scratch[:parts]
    outs = scratch[parts : 2 * parts]
    win, d, yt, zt, g, w, basis, projected, got_q, out_q, got_p, out_p = scratch[2 * parts : 2 * parts + 12]
    ssem, rsem, s2sem, r2sem, lsem, l2sem, base_sem, qsem, psem = scratch[2 * parts + 12 :]
    me = lax.axis_index("grp") * 32 + lax.axis_index("ep")
    mine = pl.ds(2 * me, 2)

    base_copy = pltpu.make_async_copy(base.at[0], d, base_sem)
    base_copy.start()

    def stored(i, k):
        block, high, wide = tile(i, CHUNKS[k])
        return adjusted.at[:, block, high, wide]

    def landed(k):
        block, high, wide = tile(me, CHUNKS[k])
        return win.at[block, high, wide]

    def own(k):
        return pltpu.make_async_copy(stored(me, k), gots[k].at[mine], lsem.at[k])

    def own2(k):
        return pltpu.make_async_copy(outs[k].at[me], landed(k), l2sem.at[k])

    for k in range(parts):
        own(k).start()
        push(lambda t, k=k: stored(t, k), lambda t, k=k: gots[k].at[mine], ssem.at[k], rsem.at[k])
    st = sketch[...].astype(F32).T.astype(BF)
    for k in range(parts):
        own(k).wait()
        wait_for(gots[k], 2 * (N - 1), rsem.at[k])

        def pick(b, car, k=k):
            outs[k][b] = gots[k][adjusted_of[b]]
            return car

        lax.fori_loop(0, N, pick, 0)
        own2(k).start()
        push(lambda t, k=k: outs[k].at[t], lambda t, k=k: landed(k), s2sem.at[k], r2sem.at[k])

    base_copy.wait()
    g[...] = jnp.zeros_like(g)

    def rows_of(c):
        return pl.ds(pl.multiple_of(c * 16, 16), 16)

    def delta(c):
        return d[:, rows_of(c), :].reshape(C, 1024)

    def first(c, car):
        apart = win[:, rows_of(c), :].reshape(C, 1024).astype(F32) - delta(c).astype(F32)
        dc = apart.astype(BF)
        d[:, rows_of(c), :] = dc.reshape(32, 16, 1024)
        y = dot(st, dc, NT)
        yt[c] = y
        g[...] += gram(y)
        return car

    for k in range(parts):
        own2(k).wait()
        wait_for(outs[k], N - 1, r2sem.at[k])
        low, rows = CHUNKS[k]
        lax.fori_loop(low // 16, (low + rows) // 16, first, 0)

    def project():
        def body(c, car):
            q = dot(wide_left(w[...]), wide_right(yt[c]), NN)
            zt[...] += dot(q.astype(BF), delta(c), NN)
            return car

        zt[...] = jnp.zeros_like(zt)
        lax.fori_loop(0, NC, body, 0)

    def step(t, car):
        chol_inv(g, w)

        @pl.when(t % 2 == 0)
        def _():
            project()
            g[...] = gram(zt[...])

        @pl.when(t % 2 == 1)
        def _():
            at = dot(wide_left(w[...]), wide_right(zt[...]), NN).astype(BF)
            g[...] = jnp.zeros_like(g)

            def back(c, car):
                y = dot(at, delta(c), NT)
                yt[c] = y
                g[...] += gram(y)
                return car

            lax.fori_loop(0, NC, back, 0)

        return car

    lax.fori_loop(0, 4, step, 0)
    chol_inv(g, w)

    def last(c, car):
        q = dot(wide_left(w[...]), wide_right(yt[c]), NN)
        basis[:, rows_of(c), :] = q.T.astype(BF).reshape(32, 16, K)
        yt[c] = q
        return car

    lax.fori_loop(0, NC, last, 0)
    relay = me < 112
    even = me % 2 == 0

    def both(condition, yes, no):
        pl.when(condition)(yes)
        pl.when(jnp.logical_not(condition))(no)

    own_q = pltpu.make_async_copy(basis_rows(basis, me), got_q.at[me], qsem.at[4])
    own_q2 = pltpu.make_async_copy(out_q.at[me], basis_rows(basis_out, me), qsem.at[5])
    own_p = pltpu.make_async_copy(projected_rows(projected, me), got_p.at[me], psem.at[4])
    own_p2 = pltpu.make_async_copy(out_p.at[me], projected_rows(projected_out, me), psem.at[5])

    push(lambda t: basis_rows(basis, t), lambda t: got_q.at[me], qsem.at[0], qsem.at[1], lambda t: t < 112)
    pl.when(relay)(own_q.start)

    zt[...] = jnp.zeros_like(zt)

    def final(c, car):
        zt[...] += dot(yt[c].astype(BF), delta(c), NN)
        return car

    lax.fori_loop(0, NC, final, 0)
    for j in range(8):
        projected[K * j : K * (j + 1), :] = zt[:, K * j : K * (j + 1)].astype(BF)
    push(lambda t: projected_rows(projected, t), lambda t: got_p.at[me], psem.at[0], psem.at[1], lambda t: t % 2 == 0)
    pl.when(even)(own_p.start)

    @pl.when(relay)
    def _():
        own_q.wait()
        wait_for(got_q, N - 1, qsem.at[1])

        def pick(b, car):
            out_q[b] = got_q[result_of[b]]
            return car

        lax.fori_loop(0, N, pick, 0)
        own_q2.start()
        push(lambda t: out_q.at[t], lambda t: basis_rows(basis_out, me), qsem.at[2], qsem.at[3])

    @pl.when(even)
    def _():
        own_p.wait()
        wait_for(got_p, N - 1, psem.at[1])

        def pick(b, car):
            out_p[b] = got_p[result_of[b]]
            return car

        lax.fori_loop(0, N, pick, 0)
        own_p2.start()
        push(lambda t: out_p.at[t], lambda t: projected_rows(projected_out, me), psem.at[2], psem.at[3])

    for k in range(parts):
        wait_for(gots[k], 2 * (N - 1), ssem.at[k])
        wait_for(outs[k], N - 1, s2sem.at[k])

    @pl.when(relay)
    def _():
        own_q2.wait()
        wait_for(out_q, 111, qsem.at[0])
        wait_for(out_q, 111, qsem.at[3])
        wait_for(out_q, N - 1, qsem.at[2])

    @pl.when(jnp.logical_not(relay))
    def _():
        wait_for(out_q, 112, qsem.at[0])
        wait_for(out_q, 112, qsem.at[3])

    @pl.when(even)
    def _():
        own_p2.wait()
        wait_for(out_p, 63, psem.at[0])
        wait_for(out_p, 63, psem.at[3])
        wait_for(out_p, N - 1, psem.at[2])

    @pl.when(jnp.logical_not(even))
    def _():
        wait_for(out_p, 64, psem.at[0])
        wait_for(out_p, 64, psem.at[3])


def relocate_and_factor(adjusted_of, result_of, adjusted, base, sketch):
    smem = pl.BlockSpec(memory_space=pltpu.SMEM)
    anywhere = pl.BlockSpec(memory_space=pl.ANY)
    parts = len(CHUNKS)
    return pl.pallas_call(
        kernel,
        out_shape=(jax.ShapeDtypeStruct((32, 112, K), BF), jax.ShapeDtypeStruct((1024, K), BF)),
        in_specs=[smem, smem, anywhere, anywhere, pl.BlockSpec(memory_space=pltpu.VMEM)],
        out_specs=(anywhere, anywhere),
        scratch_shapes=[pltpu.VMEM((2 * N, rows, 256), BF) for _, rows in CHUNKS]
        + [pltpu.VMEM((N, rows, 256), BF) for _, rows in CHUNKS]
        + [
            pltpu.VMEM((32, 112, 1024), BF),
            pltpu.VMEM((32, 112, 1024), BF),
            pltpu.VMEM((NC, K, C), F32),
            pltpu.VMEM((K, 1024), F32),
            pltpu.VMEM((K, K), F32),
            pltpu.VMEM((K, K), F32),
            pltpu.VMEM((32, 112, K), BF),
            pltpu.VMEM((1024, K), BF),
            pltpu.VMEM((N, 2, 16, K), BF),
            pltpu.VMEM((N, 2, 16, K), BF),
            pltpu.VMEM((N, 16, K), BF),
            pltpu.VMEM((N, 16, K), BF),
        ]
        + [pltpu.SemaphoreType.DMA((parts,))] * 6
        + [pltpu.SemaphoreType.DMA, pltpu.SemaphoreType.DMA((6,)), pltpu.SemaphoreType.DMA((6,))],
        compiler_params=pltpu.CompilerParams(has_side_effects=True, vmem_limit_bytes=54 * 2**20),
        name="relocate_and_factor",
    )(adjusted_of, result_of, adjusted.reshape(2, 32, 112, 1024), base.reshape(1, 32, 112, 1024), sketch)


def by_key(key, value):
    places = lax.broadcasted_iota(jnp.int32, (N, N), 0)
    return jnp.sum(jnp.where(places == key[None, :], value[None, :], 0), axis=1, dtype=jnp.int32)


def shards(base_tiles, adjusted_tiles, sketch, base_place, adjusted_place, owner_map):
    adjusted_of = by_key(base_place, adjusted_place)
    result_of = by_key(owner_map, base_place)
    basis, projected = relocate_and_factor(adjusted_of, result_of, adjusted_tiles, base_tiles, sketch)
    scaled_basis = basis.reshape(3584, K).astype(F32) * math.sqrt(3584)
    projected = projected.astype(F32).reshape(8, K, K).transpose(1, 0, 2).reshape(K, 1024)
    return (scaled_basis[None], projected[None])


def solution(mesh):
    in_specs = (P(("grp", "ep"), None, None), P(("grp", "ep"), None, None), P(), P(), P(), P())
    out_specs = (P(("grp", "ep"), None, None), P(("grp", "ep"), None, None))
    return jax.shard_map(shards, mesh=mesh, in_specs=in_specs, out_specs=out_specs, check_vma=False)
```

```python
import math

import jax
import jax.numpy as jnp
from jax import lax
from jax.experimental import pallas as pl
from jax.experimental.pallas import tpu as pltpu
from jax.sharding import PartitionSpec as P

MESH = pl.DeviceIdType.MESH
N = 128
CHUNKS = ((0, 32), (32, 32), (64, 32), (96, 16))
F32 = jnp.float32
BF = jnp.bfloat16
NT = (((1,), (1,)), ((), ()))
NN = (((1,), (0,)), ((), ()))
TN = (((0,), (0,)), ((), ()))
K = 128
BLOCK = 32
C = 512
ROWS = 3584
HALF = ROWS // 2

def dot(a, b, dims):
    return lax.dot_general(a, b, dims, preferred_element_type=F32)

def split3(v):
    hi = v.astype(BF).astype(F32)
    rest = v - hi
    mid = rest.astype(BF).astype(F32)
    return hi, mid, rest - mid


def chol_inv(g_ref, w_ref):
    sub = lax.broadcasted_iota(jnp.int32, (8, K), 0)
    a = g_ref[...]
    row = lax.broadcasted_iota(jnp.int32, (K, K), 0)
    col = lax.broadcasted_iota(jnp.int32, (K, K), 1)
    x = jnp.where(row == col, 1.0, 0.0).astype(F32)
    for b0 in range(0, K, BLOCK):
        panel = [a[i : i + 8] for i in range(0, BLOCK, 8)]
        side = [x[i : i + 8] for i in range(0, BLOCK, 8)]
        us = []
        ws = []
        for r0 in range(b0, b0 + BLOCK, 8):
            p = panel.pop(0)
            xp = side.pop(0)
            s = {}
            for i in range(8):
                for k in range(i + 1):
                    s[i, k] = jnp.broadcast_to(p[i : i + 1, r0 + k : r0 + k + 1], (8, K))
            rows = [jnp.broadcast_to(p[i : i + 1, :], (8, K)) for i in range(8)]
            xrows = [jnp.broadcast_to(xp[i : i + 1, :], (8, K)) for i in range(8)]
            below = [[jnp.broadcast_to(q[:, r0 + k : r0 + k + 1], (8, K)) for k in range(8)] for q in panel]
            u = jnp.zeros((8, K), F32)
            w = jnp.zeros((8, K), F32)
            for k in range(8):
                r = lax.rsqrt(s[k, k])
                uk = rows[k] * r
                wk = xrows[k] * r
                u = jnp.where(sub == k, uk, u)
                w = jnp.where(sub == k, wk, w)
                l = {i: s[i, k] * r for i in range(k + 1, 8)}
                for i in range(k + 1, 8):
                    for m in range(k + 1, i + 1):
                        s[i, m] = s[i, m] - l[i] * l[m]
                for i in range(k + 1, 8):
                    rows[i] = rows[i] - l[i] * uk
                    xrows[i] = xrows[i] - l[i] * wk
                for n, c in enumerate(below):
                    ck = c[k] * r
                    for m in range(k + 1, 8):
                        c[m] = c[m] - ck * l[m]
                    panel[n] = panel[n] - ck * uk
                    side[n] = side[n] - ck * wk
            w_ref[pl.ds(r0, 8), :] = w
            us.append(u)
            ws.append(w)
        if b0 < K - BLOCK:
            uh, um, ul = split3(jnp.concatenate(us, axis=0))
            wh, wm, wl = split3(jnp.concatenate(ws, axis=0))
            left = jnp.concatenate([uh, uh, um, uh, ul, um], axis=0).astype(BF)
            right = jnp.concatenate(
                [
                    jnp.concatenate([uh, um, uh, ul, uh, um], axis=0).astype(BF),
                    jnp.concatenate([wh, wm, wh, wl, wh, wm], axis=0).astype(BF),
                ],
                axis=1,
            )
            upd = dot(left, right, TN)
            a = a[BLOCK:] - upd[b0 + BLOCK :, :K]
            x = x[BLOCK:] - upd[b0 + BLOCK :, K:]


def wide_left(v):
    hi = v.astype(BF)
    return jnp.concatenate([hi, hi, (v - hi.astype(F32)).astype(BF)], axis=1)


def wide_right(v):
    hi = v.astype(BF)
    return jnp.concatenate([hi, (v - hi.astype(F32)).astype(BF), hi], axis=0)


def gram(v):
    hi, mid, low = (part.astype(BF) for part in split3(v))
    first = dot(hi, jnp.concatenate([hi, mid, low], axis=0), NT)
    cross = first[:, K : 2 * K] + first[:, 2 * K :]
    return first[:, :K] + dot(mid, mid, NT) + cross + cross.T


def peer(o):
    x = lax.axis_index("grp")
    e = lax.axis_index("ep")
    o = (o * 101) % 128
    sign = 1 - 2 * (e % 2)
    tx = (x + 4 + sign * (o // 32)) % 4
    tz = (e // 8 + 4 + sign * ((o // 8) % 4)) % 4
    ty = ((e // 2) % 4 + 4 + sign * ((o // 2) % 4)) % 4
    return tx, tz * 8 + ty * 2 + (e + o) % 2


def whole(device):
    return None


def push(src, dst, send_sem, recv_sem, when=whole):
    def one(o, car):
        tx, te = peer(o)
        t = tx * 32 + te

        def start():
            pltpu.make_async_remote_copy(
                src(t), dst(t), send_sem, recv_sem, device_id=(tx, te), device_id_type=MESH
            ).start()

        if when is whole:
            start()
        else:
            pl.when(when(t))(start)
        return car

    lax.fori_loop(1, N, one, 0)


def wait_for(ref, count, sem):
    part = ref.at[pl.ds(0, count)]
    pltpu.make_async_copy(part, part, sem).wait()


def tile(i, chunk):
    first, rows = chunk
    return i // 4, pl.ds(first, rows), pl.ds(pl.multiple_of((i % 4) * 256, 256), 256)


def basis_rows(ref, i):
    return ref.at[pl.ds((i % 16) * 2, 2), pl.ds(pl.multiple_of((i // 16) * 16, 16), 16)]


def projected_rows(ref, i):
    return ref.at[pl.ds(pl.multiple_of((i // 2) * 16, 16), 16)]


def kernel(adjusted_of, result_of, adjusted, base, sketch, basis_out, projected_out, *scratch):
    parts = len(CHUNKS)
    gots = scratch[:parts]
    outs = scratch[parts : 2 * parts]
    win, old, d, yt, zt, g, w, basis, projected, got_q, out_q, got_p, out_p = scratch[2 * parts : 2 * parts + 13]
    ssem, rsem, s2sem, r2sem, lsem, l2sem, base_sem, qsem, psem = scratch[2 * parts + 13 :]
    me = lax.axis_index("grp") * 32 + lax.axis_index("ep")
    mine = pl.ds(2 * me, 2)

    base_copy = pltpu.make_async_copy(base.at[0], old, base_sem)
    base_copy.start()

    def stored(i, k):
        block, high, wide = tile(i, CHUNKS[k])
        return adjusted.at[:, block, high, wide]

    def landed(k):
        block, high, wide = tile(me, CHUNKS[k])
        return win.at[block, high, wide]

    def own(k):
        return pltpu.make_async_copy(stored(me, k), gots[k].at[mine], lsem.at[k])

    def own2(k):
        return pltpu.make_async_copy(outs[k].at[me], landed(k), l2sem.at[k])

    for k in range(parts):
        own(k).start()
        push(lambda t, k=k: stored(t, k), lambda t, k=k: gots[k].at[mine], ssem.at[k], rsem.at[k])
    st = sketch[...].astype(F32).T.astype(BF)
    for k in range(parts):
        own(k).wait()
        wait_for(gots[k], 2 * (N - 1), rsem.at[k])

        def pick(b, car, k=k):
            outs[k][b] = gots[k][adjusted_of[b]]
            return car

        lax.fori_loop(0, N, pick, 0)
        own2(k).start()
        push(lambda t, k=k: outs[k].at[t], lambda t, k=k: landed(k), s2sem.at[k], r2sem.at[k])

    base_copy.wait()
    g[...] = jnp.zeros_like(g)

    def first(c, car):
        rows = pl.ds(pl.multiple_of(c * 16, 16), 16)
        apart = win[:, rows, :].reshape(C, 1024).astype(F32) - old[:, rows, :].reshape(C, 1024).astype(F32)
        dc = apart.astype(BF)
        here = pl.ds(pl.multiple_of(c * C, C), C)
        d[here, :] = dc
        y = dot(st, dc, NT)
        yt[:, here] = y
        g[...] += gram(y)
        return car

    for k in range(parts):
        own2(k).wait()
        wait_for(outs[k], N - 1, r2sem.at[k])
        low, rows = CHUNKS[k]
        lax.fori_loop(low // 16, (low + rows) // 16, first, 0)

    halves = (pl.ds(0, HALF), pl.ds(HALF, HALF))

    def step(t, car):
        chol_inv(g, w)
        left = wide_left(w[...])

        @pl.when(t % 2 == 0)
        def _():
            total = jnp.zeros((K, 1024), F32)
            for h in halves:
                q = dot(left, wide_right(yt[:, h]), NN)
                total = total + dot(q.astype(BF), d[h, :], NN)
            zt[...] = total
            g[...] = gram(total)

        @pl.when(t % 2 == 1)
        def _():
            across = dot(left, wide_right(zt[...]), NN).astype(BF)
            total = jnp.zeros((K, K), F32)
            for h in halves:
                y = dot(across, d[h, :], NT)
                yt[:, h] = y
                total = total + gram(y)
            g[...] = total

        return car

    lax.fori_loop(0, 4, step, 0)
    chol_inv(g, w)

    left = wide_left(w[...])
    for n, h in enumerate(halves):
        q = dot(left, wide_right(yt[:, h]), NN)
        basis[56 * n : 56 * (n + 1)] = q.T.astype(BF).reshape(56, 2, 16, K)
        yt[:, h] = q
    relay = me < 112
    even = me % 2 == 0

    def both(condition, yes, no):
        pl.when(condition)(yes)
        pl.when(jnp.logical_not(condition))(no)

    own_q = pltpu.make_async_copy(basis.at[me % 112], got_q.at[me], qsem.at[4])
    own_q2 = pltpu.make_async_copy(out_q.at[me], basis_rows(basis_out, me), qsem.at[5])
    own_p = pltpu.make_async_copy(projected_rows(projected, me), got_p.at[me], psem.at[4])
    own_p2 = pltpu.make_async_copy(out_p.at[me], projected_rows(projected_out, me), psem.at[5])

    push(lambda t: basis.at[t], lambda t: got_q.at[me], qsem.at[0], qsem.at[1], lambda t: t < 112)
    pl.when(relay)(own_q.start)

    total = jnp.zeros((K, 1024), F32)
    for h in halves:
        total = total + dot(yt[:, h].astype(BF), d[h, :], NN)
    for j in range(8):
        projected[K * j : K * (j + 1), :] = total[:, K * j : K * (j + 1)].astype(BF)
    push(lambda t: projected_rows(projected, t), lambda t: got_p.at[me], psem.at[0], psem.at[1], lambda t: t % 2 == 0)
    pl.when(even)(own_p.start)

    @pl.when(relay)
    def _():
        own_q.wait()
        wait_for(got_q, N - 1, qsem.at[1])

        def pick(b, car):
            out_q[b] = got_q[result_of[b]]
            return car

        lax.fori_loop(0, N, pick, 0)
        own_q2.start()
        push(lambda t: out_q.at[t], lambda t: basis_rows(basis_out, me), qsem.at[2], qsem.at[3])

    @pl.when(even)
    def _():
        own_p.wait()
        wait_for(got_p, N - 1, psem.at[1])

        def pick(b, car):
            out_p[b] = got_p[result_of[b]]
            return car

        lax.fori_loop(0, N, pick, 0)
        own_p2.start()
        push(lambda t: out_p.at[t], lambda t: projected_rows(projected_out, me), psem.at[2], psem.at[3])

    for k in range(parts):
        wait_for(gots[k], 2 * (N - 1), ssem.at[k])
        wait_for(outs[k], N - 1, s2sem.at[k])

    @pl.when(relay)
    def _():
        own_q2.wait()
        wait_for(out_q, 111, qsem.at[0])
        wait_for(out_q, 111, qsem.at[3])
        wait_for(out_q, N - 1, qsem.at[2])

    @pl.when(jnp.logical_not(relay))
    def _():
        wait_for(out_q, 112, qsem.at[0])
        wait_for(out_q, 112, qsem.at[3])

    @pl.when(even)
    def _():
        own_p2.wait()
        wait_for(out_p, 63, psem.at[0])
        wait_for(out_p, 63, psem.at[3])
        wait_for(out_p, N - 1, psem.at[2])

    @pl.when(jnp.logical_not(even))
    def _():
        wait_for(out_p, 64, psem.at[0])
        wait_for(out_p, 64, psem.at[3])


def relocate_and_factor(adjusted_of, result_of, adjusted, base, sketch):
    smem = pl.BlockSpec(memory_space=pltpu.SMEM)
    anywhere = pl.BlockSpec(memory_space=pl.ANY)
    parts = len(CHUNKS)
    return pl.pallas_call(
        kernel,
        out_shape=(jax.ShapeDtypeStruct((32, 112, K), BF), jax.ShapeDtypeStruct((1024, K), BF)),
        in_specs=[smem, smem, anywhere, anywhere, pl.BlockSpec(memory_space=pltpu.VMEM)],
        out_specs=(anywhere, anywhere),
        scratch_shapes=[pltpu.VMEM((2 * N, rows, 256), BF) for _, rows in CHUNKS]
        + [pltpu.VMEM((N, rows, 256), BF) for _, rows in CHUNKS]
        + [
            pltpu.VMEM((32, 112, 1024), BF),
            pltpu.VMEM((32, 112, 1024), BF),
            pltpu.VMEM((ROWS, 1024), BF),
            pltpu.VMEM((K, ROWS), F32),
            pltpu.VMEM((K, 1024), F32),
            pltpu.VMEM((K, K), F32),
            pltpu.VMEM((K, K), F32),
            pltpu.VMEM((112, 2, 16, K), BF),
            pltpu.VMEM((1024, K), BF),
            pltpu.VMEM((N, 2, 16, K), BF),
            pltpu.VMEM((N, 2, 16, K), BF),
            pltpu.VMEM((N, 16, K), BF),
            pltpu.VMEM((N, 16, K), BF),
        ]
        + [pltpu.SemaphoreType.DMA((parts,))] * 6
        + [pltpu.SemaphoreType.DMA, pltpu.SemaphoreType.DMA((6,)), pltpu.SemaphoreType.DMA((6,))],
        compiler_params=pltpu.CompilerParams(has_side_effects=True, vmem_limit_bytes=58 * 2**20),
        name="relocate_and_factor",
    )(adjusted_of, result_of, adjusted.reshape(2, 32, 112, 1024), base.reshape(1, 32, 112, 1024), sketch)


def by_key(key, value):
    places = lax.broadcasted_iota(jnp.int32, (N, N), 0)
    return jnp.sum(jnp.where(places == key[None, :], value[None, :], 0), axis=1, dtype=jnp.int32)


def shards(base_tiles, adjusted_tiles, sketch, base_place, adjusted_place, owner_map):
    adjusted_of = by_key(base_place, adjusted_place)
    result_of = by_key(owner_map, base_place)
    basis, projected = relocate_and_factor(adjusted_of, result_of, adjusted_tiles, base_tiles, sketch)
    scaled_basis = basis.reshape(ROWS, K).astype(F32) * math.sqrt(ROWS)
    projected = projected.astype(F32).reshape(8, K, K).transpose(1, 0, 2).reshape(K, 1024)
    return (scaled_basis[None], projected[None])


def solution(mesh):
    in_specs = (P(("grp", "ep"), None, None), P(("grp", "ep"), None, None), P(), P(), P(), P())
    out_specs = (P(("grp", "ep"), None, None), P(("grp", "ep"), None, None))
    return jax.shard_map(shards, mesh=mesh, in_specs=in_specs, out_specs=out_specs, check_vma=False)
```

```python
import math

import jax
import jax.numpy as jnp
from jax import lax
from jax.experimental import pallas as pl
from jax.experimental.pallas import tpu as pltpu
from jax.sharding import PartitionSpec as P

MESH = pl.DeviceIdType.MESH
N = 128
CHUNKS = ((0, 32), (32, 32), (64, 32), (96, 16))
F32 = jnp.float32
BF = jnp.bfloat16
NT = (((1,), (1,)), ((), ()))
NN = (((1,), (0,)), ((), ()))
TN = (((0,), (0,)), ((), ()))
K = 128
BLOCK = 32
C = 512
ROWS = 3584
HALF = ROWS // 2

def dot(a, b, dims):
    return lax.dot_general(a, b, dims, preferred_element_type=F32)

def split3(v):
    hi = v.astype(BF).astype(F32)
    rest = v - hi
    mid = rest.astype(BF).astype(F32)
    return hi, mid, rest - mid


def chol_inv(g_ref, w_ref, t_ref):
    sub = lax.broadcasted_iota(jnp.int32, (8, K), 0)
    a = g_ref[...]
    row = lax.broadcasted_iota(jnp.int32, (K, K), 0)
    col = lax.broadcasted_iota(jnp.int32, (K, K), 1)
    x = jnp.where(row == col, 1.0, 0.0).astype(F32)
    for b0 in range(0, K, BLOCK):
        panel = [a[i : i + 8] for i in range(0, BLOCK, 8)]
        side = [x[i : i + 8] for i in range(0, BLOCK, 8)]
        us = []
        ws = []
        for r0 in range(b0, b0 + BLOCK, 8):
            p = panel.pop(0)
            xp = side.pop(0)
            s = {}
            held = t_ref.at[r0 // 8 % 2]
            for k in range(8):
                held[k] = jnp.broadcast_to(p[:, r0 + k : r0 + k + 1], (8, K))
            held[8] = p
            held[9] = xp
            for i in range(8):
                for k in range(i + 1):
                    s[i, k] = jnp.broadcast_to(held[k, i : i + 1, :], (8, K))
            rows = [jnp.broadcast_to(held[8, i : i + 1, :], (8, K)) for i in range(8)]
            xrows = [jnp.broadcast_to(held[9, i : i + 1, :], (8, K)) for i in range(8)]
            below = [[jnp.broadcast_to(q[:, r0 + k : r0 + k + 1], (8, K)) for k in range(8)] for q in panel]
            u = jnp.zeros((8, K), F32)
            w = jnp.zeros((8, K), F32)
            for k in range(8):
                r = lax.rsqrt(s[k, k])
                uk = rows[k] * r
                wk = xrows[k] * r
                u = jnp.where(sub == k, uk, u)
                w = jnp.where(sub == k, wk, w)
                l = {i: s[i, k] * r for i in range(k + 1, 8)}
                for i in range(k + 1, 8):
                    for m in range(k + 1, i + 1):
                        s[i, m] = s[i, m] - l[i] * l[m]
                for i in range(k + 1, 8):
                    rows[i] = rows[i] - l[i] * uk
                    xrows[i] = xrows[i] - l[i] * wk
                for n, c in enumerate(below):
                    ck = c[k] * r
                    for m in range(k + 1, 8):
                        c[m] = c[m] - ck * l[m]
                    panel[n] = panel[n] - ck * uk
                    side[n] = side[n] - ck * wk
            w_ref[pl.ds(r0, 8), :] = w
            us.append(u)
            ws.append(w)
        if b0 < K - BLOCK:
            uh, um, ul = split3(jnp.concatenate(us, axis=0))
            wh, wm, wl = split3(jnp.concatenate(ws, axis=0))
            left = jnp.concatenate([uh, uh, um, uh, ul, um], axis=0).astype(BF)
            right = jnp.concatenate(
                [
                    jnp.concatenate([uh, um, uh, ul, uh, um], axis=0).astype(BF),
                    jnp.concatenate([wh, wm, wh, wl, wh, wm], axis=0).astype(BF),
                ],
                axis=1,
            )
            upd = dot(left, right, TN)
            a = a[BLOCK:] - upd[b0 + BLOCK :, :K]
            x = x[BLOCK:] - upd[b0 + BLOCK :, K:]


def wide_left(v):
    hi = v.astype(BF)
    return jnp.concatenate([hi, hi, (v - hi.astype(F32)).astype(BF)], axis=1)


def wide_right(v):
    hi = v.astype(BF)
    return jnp.concatenate([hi, (v - hi.astype(F32)).astype(BF), hi], axis=0)


def gram(v):
    hi, mid, low = (part.astype(BF) for part in split3(v))
    first = dot(hi, jnp.concatenate([hi, mid, low], axis=0), NT)
    cross = first[:, K : 2 * K] + first[:, 2 * K :]
    return first[:, :K] + dot(mid, mid, NT) + cross + cross.T


def peer(o):
    x = lax.axis_index("grp")
    e = lax.axis_index("ep")
    o = lax.rem(o * 101, 128)
    sign = 1 - 2 * lax.rem(e, 2)
    tx = lax.rem(x + 4 + sign * lax.div(o, 32), 4)
    tz = lax.rem(lax.div(e, 8) + 4 + sign * lax.rem(lax.div(o, 8), 4), 4)
    ty = lax.rem(lax.rem(lax.div(e, 2), 4) + 4 + sign * lax.rem(lax.div(o, 2), 4), 4)
    return tx, tz * 8 + ty * 2 + lax.rem(e + o, 2)


def whole(device):
    return None


def push(src, dst, send_sem, recv_sem, when=whole):
    def one(o, car):
        tx, te = peer(o)
        t = tx * 32 + te

        def start():
            pltpu.make_async_remote_copy(
                src(t), dst(t), send_sem, recv_sem, device_id=(tx, te), device_id_type=MESH
            ).start()

        if when is whole:
            start()
        else:
            pl.when(when(t))(start)
        return car

    lax.fori_loop(1, N, one, 0, unroll=3)


def wait_for(ref, count, sem):
    part = ref.at[pl.ds(0, count)]
    pltpu.make_async_copy(part, part, sem).wait()


def tile(i, chunk):
    first, rows = chunk
    return i // 4, pl.ds(first, rows), pl.ds(pl.multiple_of((i % 4) * 256, 256), 256)


def entry(i):
    return lax.rem(i * 37, N)


def basis_rows(ref, n):
    return ref.at[pl.ds(lax.rem(n, 16) * 2, 2), pl.ds(pl.multiple_of(lax.div(n, 16) * 16, 16), 16)]


def projected_rows(ref, i):
    return ref.at[pl.ds(pl.multiple_of((i // 2) * 16, 16), 16)]


def kernel(adjusted_of, result_of, adjusted, base, sketch, basis_out, projected_out, *scratch):
    parts = len(CHUNKS)
    gots = scratch[:parts]
    outs = scratch[parts : 2 * parts]
    win, old, d, yt, zt, g, w, spread, basis, projected, got_q, out_q, got_p, out_p = scratch[2 * parts : 2 * parts + 14]
    ssem, rsem, s2sem, r2sem, lsem, l2sem, base_sem, qsem, psem = scratch[2 * parts + 14 :]
    me = lax.axis_index("grp") * 32 + lax.axis_index("ep")
    mine = pl.ds(2 * me, 2)

    base_copy = pltpu.make_async_copy(base.at[0], old, base_sem)
    base_copy.start()

    def stored(i, k):
        block, high, wide = tile(i, CHUNKS[k])
        return adjusted.at[:, block, high, wide]

    def landed(k):
        block, high, wide = tile(me, CHUNKS[k])
        return win.at[block, high, wide]

    def own(k):
        return pltpu.make_async_copy(stored(me, k), gots[k].at[mine], lsem.at[k])

    def own2(k):
        return pltpu.make_async_copy(outs[k].at[me], landed(k), l2sem.at[k])

    for k in range(parts):
        own(k).start()
        push(lambda t, k=k: stored(t, k), lambda t, k=k: gots[k].at[mine], ssem.at[k], rsem.at[k])
    st = sketch[...].astype(F32).T.astype(BF)
    for k in range(parts):
        own(k).wait()
        wait_for(gots[k], 2 * (N - 1), rsem.at[k])

        def pick(b, car, k=k):
            outs[k][b] = gots[k][adjusted_of[b]]
            return car

        lax.fori_loop(0, N, pick, 0, unroll=4)
        own2(k).start()
        push(lambda t, k=k: outs[k].at[t], lambda t, k=k: landed(k), s2sem.at[k], r2sem.at[k])

    base_copy.wait()
    g[...] = jnp.zeros_like(g)

    def first(c, car):
        rows = pl.ds(pl.multiple_of(c * 16, 16), 16)
        apart = win[:, rows, :].reshape(C, 1024).astype(F32) - old[:, rows, :].reshape(C, 1024).astype(F32)
        dc = apart.astype(BF)
        here = pl.ds(pl.multiple_of(c * C, C), C)
        d[here, :] = dc
        y = dot(st, dc, NT)
        yt[:, here] = y
        g[...] += gram(y)
        return car

    for k in range(parts):
        own2(k).wait()
        wait_for(outs[k], N - 1, r2sem.at[k])
        low, rows = CHUNKS[k]
        lax.fori_loop(low // 16, (low + rows) // 16, first, 0)

    halves = (pl.ds(0, HALF), pl.ds(HALF, HALF))

    def step(t, car):
        chol_inv(g, w, spread)
        left = wide_left(w[...])

        @pl.when(t % 2 == 0)
        def _():
            total = jnp.zeros((K, 1024), F32)
            for h in halves:
                q = dot(left, wide_right(yt[:, h]), NN)
                total = total + dot(q.astype(BF), d[h, :], NN)
            zt[...] = total
            g[...] = gram(total)

        @pl.when(t % 2 == 1)
        def _():
            across = dot(left, wide_right(zt[...]), NN).astype(BF)
            total = jnp.zeros((K, K), F32)
            for h in halves:
                y = dot(across, d[h, :], NT)
                yt[:, h] = y
                total = total + gram(y)
            g[...] = total

        return car

    lax.fori_loop(0, 4, step, 0)
    chol_inv(g, w, spread)

    left = wide_left(w[...])
    for n, h in enumerate(halves):
        q = dot(left, wide_right(yt[:, h]), NN)
        basis[56 * n : 56 * (n + 1)] = q.T.astype(BF).reshape(56, 2, 16, K)
        yt[:, h] = q
    place = entry(me)
    relay = place < 112
    even = me % 2 == 0

    def both(condition, yes, no):
        pl.when(condition)(yes)
        pl.when(jnp.logical_not(condition))(no)

    own_q = pltpu.make_async_copy(basis.at[lax.rem(place, 112)], got_q.at[me], qsem.at[4])
    own_q2 = pltpu.make_async_copy(out_q.at[me], basis_rows(basis_out, place), qsem.at[5])
    own_p = pltpu.make_async_copy(projected_rows(projected, me), got_p.at[me], psem.at[4])
    own_p2 = pltpu.make_async_copy(out_p.at[me], projected_rows(projected_out, me), psem.at[5])

    push(lambda t: basis.at[entry(t)], lambda t: got_q.at[me], qsem.at[0], qsem.at[1], lambda t: entry(t) < 112)
    pl.when(relay)(own_q.start)

    total = jnp.zeros((K, 1024), F32)
    for h in halves:
        total = total + dot(yt[:, h].astype(BF), d[h, :], NN)
    for j in range(8):
        projected[K * j : K * (j + 1), :] = total[:, K * j : K * (j + 1)].astype(BF)
    push(lambda t: projected_rows(projected, t), lambda t: got_p.at[me], psem.at[0], psem.at[1], lambda t: t % 2 == 0)
    pl.when(even)(own_p.start)

    @pl.when(relay)
    def _():
        own_q.wait()
        wait_for(got_q, N - 1, qsem.at[1])

        def pick(b, car):
            out_q[b] = got_q[result_of[b]]
            return car

        lax.fori_loop(0, N, pick, 0, unroll=4)
        own_q2.start()
        push(lambda t: out_q.at[t], lambda t: basis_rows(basis_out, place), qsem.at[2], qsem.at[3])

    @pl.when(even)
    def _():
        own_p.wait()
        wait_for(got_p, N - 1, psem.at[1])

        def pick(b, car):
            out_p[b] = got_p[result_of[b]]
            return car

        lax.fori_loop(0, N, pick, 0, unroll=4)
        own_p2.start()
        push(lambda t: out_p.at[t], lambda t: projected_rows(projected_out, me), psem.at[2], psem.at[3])

    for k in range(parts):
        wait_for(gots[k], 2 * (N - 1), ssem.at[k])
        wait_for(outs[k], N - 1, s2sem.at[k])

    @pl.when(relay)
    def _():
        own_q2.wait()
        wait_for(out_q, 111, qsem.at[0])
        wait_for(out_q, 111, qsem.at[3])
        wait_for(out_q, N - 1, qsem.at[2])

    @pl.when(jnp.logical_not(relay))
    def _():
        wait_for(out_q, 112, qsem.at[0])
        wait_for(out_q, 112, qsem.at[3])

    @pl.when(even)
    def _():
        own_p2.wait()
        wait_for(out_p, 63, psem.at[0])
        wait_for(out_p, 63, psem.at[3])
        wait_for(out_p, N - 1, psem.at[2])

    @pl.when(jnp.logical_not(even))
    def _():
        wait_for(out_p, 64, psem.at[0])
        wait_for(out_p, 64, psem.at[3])


def relocate_and_factor(adjusted_of, result_of, adjusted, base, sketch):
    smem = pl.BlockSpec(memory_space=pltpu.SMEM)
    anywhere = pl.BlockSpec(memory_space=pl.ANY)
    parts = len(CHUNKS)
    return pl.pallas_call(
        kernel,
        out_shape=(jax.ShapeDtypeStruct((32, 112, K), BF), jax.ShapeDtypeStruct((1024, K), BF)),
        in_specs=[smem, smem, anywhere, anywhere, pl.BlockSpec(memory_space=pltpu.VMEM)],
        out_specs=(anywhere, anywhere),
        scratch_shapes=[pltpu.VMEM((2 * N, rows, 256), BF) for _, rows in CHUNKS]
        + [pltpu.VMEM((N, rows, 256), BF) for _, rows in CHUNKS]
        + [
            pltpu.VMEM((32, 112, 1024), BF),
            pltpu.VMEM((32, 112, 1024), BF),
            pltpu.VMEM((ROWS, 1024), BF),
            pltpu.VMEM((K, ROWS), F32),
            pltpu.VMEM((K, 1024), F32),
            pltpu.VMEM((K, K), F32),
            pltpu.VMEM((K, K), F32),
            pltpu.VMEM((2, 10, 8, K), F32),
            pltpu.VMEM((112, 2, 16, K), BF),
            pltpu.VMEM((1024, K), BF),
            pltpu.VMEM((N, 2, 16, K), BF),
            pltpu.VMEM((N, 2, 16, K), BF),
            pltpu.VMEM((N, 16, K), BF),
            pltpu.VMEM((N, 16, K), BF),
        ]
        + [pltpu.SemaphoreType.DMA((parts,))] * 6
        + [pltpu.SemaphoreType.DMA, pltpu.SemaphoreType.DMA((6,)), pltpu.SemaphoreType.DMA((6,))],
        compiler_params=pltpu.CompilerParams(has_side_effects=True, vmem_limit_bytes=58 * 2**20),
        name="relocate_and_factor",
    )(adjusted_of, result_of, adjusted.reshape(2, 32, 112, 1024), base.reshape(1, 32, 112, 1024), sketch)


def by_key(key, value):
    places = lax.broadcasted_iota(jnp.int32, (N, N), 0)
    return jnp.sum(jnp.where(places == key[None, :], value[None, :], 0), axis=1, dtype=jnp.int32)


def shards(base_tiles, adjusted_tiles, sketch, base_place, adjusted_place, owner_map):
    adjusted_of = by_key(base_place, adjusted_place)
    result_of = by_key(owner_map, base_place)
    basis, projected = relocate_and_factor(adjusted_of, result_of, adjusted_tiles, base_tiles, sketch)
    scaled_basis = basis.reshape(ROWS, K).astype(F32) * math.sqrt(ROWS)
    projected = projected.astype(F32).reshape(8, K, K).transpose(1, 0, 2).reshape(K, 1024)
    return (scaled_basis[None], projected[None])


def solution(mesh):
    in_specs = (P(("grp", "ep"), None, None), P(("grp", "ep"), None, None), P(), P(), P(), P())
    out_specs = (P(("grp", "ep"), None, None), P(("grp", "ep"), None, None))
    return jax.shard_map(shards, mesh=mesh, in_specs=in_specs, out_specs=out_specs, check_vma=False)
```

```python
import math

import jax
import jax.numpy as jnp
from jax import lax
from jax.experimental import pallas as pl
from jax.experimental.pallas import tpu as pltpu
from jax.sharding import PartitionSpec as P

MESH = pl.DeviceIdType.MESH
N = 128
CHUNKS = ((0, 32), (32, 32), (64, 32), (96, 16))
F32 = jnp.float32
BF = jnp.bfloat16
NT = (((1,), (1,)), ((), ()))
NN = (((1,), (0,)), ((), ()))
TN = (((0,), (0,)), ((), ()))
K = 128
BLOCK = 32
C = 512
ROWS = 3584
HALF = ROWS // 2

def dot(a, b, dims):
    return lax.dot_general(a, b, dims, preferred_element_type=F32)

def split3(v):
    hi = v.astype(BF).astype(F32)
    rest = v - hi
    mid = rest.astype(BF).astype(F32)
    return hi, mid, rest - mid


def chol_inv(g_ref, w_ref, t_ref):
    sub = lax.broadcasted_iota(jnp.int32, (8, K), 0)
    a = g_ref[...]
    row = lax.broadcasted_iota(jnp.int32, (K, K), 0)
    col = lax.broadcasted_iota(jnp.int32, (K, K), 1)
    x = jnp.where(row == col, 1.0, 0.0).astype(F32)
    for b0 in range(0, K, BLOCK):
        panel = [a[i : i + 8] for i in range(0, BLOCK, 8)]
        side = [x[i : i + 8] for i in range(0, BLOCK, 8)]
        us = []
        ws = []
        for r0 in range(b0, b0 + BLOCK, 8):
            p = panel.pop(0)
            xp = side.pop(0)
            s = {}
            held = t_ref.at[r0 // 8 % 2]
            for k in range(8):
                held[k] = jnp.broadcast_to(p[:, r0 + k : r0 + k + 1], (8, K))
            held[8] = p
            held[9] = xp
            for i in range(8):
                for k in range(i + 1):
                    s[i, k] = jnp.broadcast_to(held[k, i : i + 1, :], (8, K))
            rows = [jnp.broadcast_to(held[8, i : i + 1, :], (8, K)) for i in range(8)]
            xrows = [jnp.broadcast_to(held[9, i : i + 1, :], (8, K)) for i in range(8)]
            below = [[jnp.broadcast_to(q[:, r0 + k : r0 + k + 1], (8, K)) for k in range(8)] for q in panel]
            u = jnp.zeros((8, K), F32)
            w = jnp.zeros((8, K), F32)
            for k in range(8):
                r = lax.rsqrt(s[k, k])
                uk = rows[k] * r
                wk = xrows[k] * r
                u = jnp.where(sub == k, uk, u)
                w = jnp.where(sub == k, wk, w)
                l = {i: s[i, k] * r for i in range(k + 1, 8)}
                for i in range(k + 1, 8):
                    for m in range(k + 1, i + 1):
                        s[i, m] = s[i, m] - l[i] * l[m]
                for i in range(k + 1, 8):
                    rows[i] = rows[i] - l[i] * uk
                    xrows[i] = xrows[i] - l[i] * wk
                for n, c in enumerate(below):
                    ck = c[k] * r
                    for m in range(k + 1, 8):
                        c[m] = c[m] - ck * l[m]
                    panel[n] = panel[n] - ck * uk
                    side[n] = side[n] - ck * wk
            w_ref[pl.ds(r0, 8), :] = w
            us.append(u)
            ws.append(w)
        if b0 < K - BLOCK:
            uh, um, ul = split3(jnp.concatenate(us, axis=0))
            wh, wm, wl = split3(jnp.concatenate(ws, axis=0))
            left = jnp.concatenate([uh, uh, um, uh, ul, um], axis=0).astype(BF)
            right = jnp.concatenate(
                [
                    jnp.concatenate([uh, um, uh, ul, uh, um], axis=0).astype(BF),
                    jnp.concatenate([wh, wm, wh, wl, wh, wm], axis=0).astype(BF),
                ],
                axis=1,
            )
            upd = dot(left, right, TN)
            a = a[BLOCK:] - upd[b0 + BLOCK :, :K]
            x = x[BLOCK:] - upd[b0 + BLOCK :, K:]


def wide_left(v):
    hi = v.astype(BF)
    return jnp.concatenate([hi, hi, (v - hi.astype(F32)).astype(BF)], axis=1)


def wide_right(v):
    hi = v.astype(BF)
    return jnp.concatenate([hi, (v - hi.astype(F32)).astype(BF), hi], axis=0)


def gram(v):
    hi, mid, low = (part.astype(BF) for part in split3(v))
    first = dot(hi, jnp.concatenate([hi, mid, low], axis=0), NT)
    cross = first[:, K : 2 * K] + first[:, 2 * K :]
    return first[:, :K] + dot(mid, mid, NT) + cross + cross.T


def peer(o):
    x = lax.axis_index("grp")
    e = lax.axis_index("ep")
    o = lax.rem(o * 101, 128)
    sign = 1 - 2 * lax.rem(e, 2)
    tx = lax.rem(x + 4 + sign * lax.div(o, 32), 4)
    tz = lax.rem(lax.div(e, 8) + 4 + sign * lax.rem(lax.div(o, 8), 4), 4)
    ty = lax.rem(lax.rem(lax.div(e, 2), 4) + 4 + sign * lax.rem(lax.div(o, 2), 4), 4)
    return tx, tz * 8 + ty * 2 + lax.rem(e + o, 2)


def whole(device):
    return None


def push(src, dst, send_sem, recv_sem, when=whole):
    def one(o, car):
        tx, te = peer(o)
        t = tx * 32 + te

        def start():
            pltpu.make_async_remote_copy(
                src(t), dst(t), send_sem, recv_sem, device_id=(tx, te), device_id_type=MESH
            ).start()

        if when is whole:
            start()
        else:
            pl.when(when(t))(start)
        return car

    lax.fori_loop(1, N, one, 0, unroll=3)


def wait_for(ref, count, sem):
    part = ref.at[pl.ds(0, count)]
    pltpu.make_async_copy(part, part, sem).wait()


def tile(i, chunk):
    first, rows = chunk
    return i // 4, pl.ds(first, rows), pl.ds(pl.multiple_of((i % 4) * 256, 256), 256)


def entry(i):
    return lax.rem(i * 37, N)


def basis_rows(ref, n):
    return ref.at[pl.ds(lax.rem(n, 16) * 2, 2), pl.ds(pl.multiple_of(lax.div(n, 16) * 16, 16), 16)]


def projected_rows(ref, i):
    return ref.at[pl.ds(pl.multiple_of((i // 2) * 16, 16), 16)]


def kernel(adjusted_of, result_of, adjusted, base, sketch, basis_out, projected_out, *scratch):
    parts = len(CHUNKS)
    gots = scratch[:parts]
    outs = scratch[parts : 2 * parts]
    win, d, yt, zt, g, w, spread, basis, projected, got_q, out_q, got_p, out_p = scratch[2 * parts : 2 * parts + 13]
    ssem, rsem, s2sem, r2sem, lsem, l2sem, base_sem, qsem, psem = scratch[2 * parts + 13 :]
    me = lax.axis_index("grp") * 32 + lax.axis_index("ep")
    mine = pl.ds(2 * me, 2)

    base_copies = [
        pltpu.make_async_copy(base.at[0, :, pl.ds(16 * c, 16)], d.at[pl.ds(32 * c, 32)], base_sem.at[c]) for c in range(7)
    ]
    for copy in base_copies:
        copy.start()

    def stored(i, k):
        block, high, wide = tile(i, CHUNKS[k])
        return adjusted.at[:, block, high, wide]

    def landed(k):
        block, high, wide = tile(me, CHUNKS[k])
        return win.at[block, high, wide]

    def own(k):
        return pltpu.make_async_copy(stored(me, k), gots[k].at[mine], lsem.at[k])

    def own2(k):
        return pltpu.make_async_copy(outs[k].at[me], landed(k), l2sem.at[k])

    for k in range(parts):
        own(k).start()
        push(lambda t, k=k: stored(t, k), lambda t, k=k: gots[k].at[mine], ssem.at[k], rsem.at[k])
    st = sketch[...].astype(F32).T.astype(BF)
    for k in range(parts):
        own(k).wait()
        wait_for(gots[k], 2 * (N - 1), rsem.at[k])

        def pick(b, car, k=k):
            outs[k][b] = gots[k][adjusted_of[b]]
            return car

        lax.fori_loop(0, N, pick, 0, unroll=4)
        own2(k).start()
        push(lambda t, k=k: outs[k].at[t], lambda t, k=k: landed(k), s2sem.at[k], r2sem.at[k])

    for copy in base_copies:
        copy.wait()
    g[...] = jnp.zeros_like(g)

    def first(c, car):
        rows = pl.ds(pl.multiple_of(c * 16, 16), 16)
        held = pl.ds(pl.multiple_of(c * 32, 32), 32)
        here = pl.ds(pl.multiple_of(c * C, C), C)
        dc = (win[:, rows, :].astype(F32) - d[held].astype(F32)).astype(BF)
        d[held] = dc
        dc = dc.reshape(C, 1024)
        y = dot(st, dc, NT)
        yt[:, here] = y
        g[...] += gram(y)
        return car

    for k in range(parts):
        own2(k).wait()
        wait_for(outs[k], N - 1, r2sem.at[k])
        low, rows = CHUNKS[k]
        lax.fori_loop(low // 16, (low + rows) // 16, first, 0)

    halves = (pl.ds(0, HALF), pl.ds(HALF, HALF))

    def delta(n):
        return d[112 * n : 112 * (n + 1)].reshape(HALF, 1024)

    def step(t, car):
        chol_inv(g, w, spread)
        left = wide_left(w[...])

        @pl.when(t % 2 == 0)
        def _():
            total = jnp.zeros((K, 1024), F32)
            for n, h in enumerate(halves):
                q = dot(left, wide_right(yt[:, h]), NN)
                total = total + dot(q.astype(BF), delta(n), NN)
            zt[...] = total
            g[...] = gram(total)

        @pl.when(t % 2 == 1)
        def _():
            across = dot(left, wide_right(zt[...]), NN).astype(BF)
            total = jnp.zeros((K, K), F32)
            for n, h in enumerate(halves):
                y = dot(across, delta(n), NT)
                yt[:, h] = y
                total = total + gram(y)
            g[...] = total

        return car

    lax.fori_loop(0, 4, step, 0)
    chol_inv(g, w, spread)

    left = wide_left(w[...])
    for n, h in enumerate(halves):
        q = dot(left, wide_right(yt[:, h]), NN)
        basis[56 * n : 56 * (n + 1)] = q.T.astype(BF).reshape(56, 2, 16, K)
        yt[:, h] = q
    place = entry(me)
    relay = place < 112
    even = me % 2 == 0

    def both(condition, yes, no):
        pl.when(condition)(yes)
        pl.when(jnp.logical_not(condition))(no)

    own_q = pltpu.make_async_copy(basis.at[lax.rem(place, 112)], got_q.at[me], qsem.at[4])
    own_q2 = pltpu.make_async_copy(out_q.at[me], basis_rows(basis_out, place), qsem.at[5])
    own_p = pltpu.make_async_copy(projected_rows(projected, me), got_p.at[me], psem.at[4])
    own_p2 = pltpu.make_async_copy(out_p.at[me], projected_rows(projected_out, me), psem.at[5])

    push(lambda t: basis.at[entry(t)], lambda t: got_q.at[me], qsem.at[0], qsem.at[1], lambda t: entry(t) < 112)
    pl.when(relay)(own_q.start)

    total = jnp.zeros((K, 1024), F32)
    for n, h in enumerate(halves):
        total = total + dot(yt[:, h].astype(BF), delta(n), NN)
    for j in range(8):
        projected[K * j : K * (j + 1), :] = total[:, K * j : K * (j + 1)].astype(BF)
    push(lambda t: projected_rows(projected, t), lambda t: got_p.at[me], psem.at[0], psem.at[1], lambda t: t % 2 == 0)
    pl.when(even)(own_p.start)

    @pl.when(relay)
    def _():
        own_q.wait()
        wait_for(got_q, N - 1, qsem.at[1])

        def pick(b, car):
            out_q[b] = got_q[result_of[b]]
            return car

        lax.fori_loop(0, N, pick, 0, unroll=4)
        own_q2.start()
        push(lambda t: out_q.at[t], lambda t: basis_rows(basis_out, place), qsem.at[2], qsem.at[3])

    @pl.when(even)
    def _():
        own_p.wait()
        wait_for(got_p, N - 1, psem.at[1])

        def pick(b, car):
            out_p[b] = got_p[result_of[b]]
            return car

        lax.fori_loop(0, N, pick, 0, unroll=4)
        own_p2.start()
        push(lambda t: out_p.at[t], lambda t: projected_rows(projected_out, me), psem.at[2], psem.at[3])

    for k in range(parts):
        wait_for(gots[k], 2 * (N - 1), ssem.at[k])
        wait_for(outs[k], N - 1, s2sem.at[k])

    @pl.when(relay)
    def _():
        own_q2.wait()
        wait_for(out_q, 111, qsem.at[0])
        wait_for(out_q, 111, qsem.at[3])
        wait_for(out_q, N - 1, qsem.at[2])

    @pl.when(jnp.logical_not(relay))
    def _():
        wait_for(out_q, 112, qsem.at[0])
        wait_for(out_q, 112, qsem.at[3])

    @pl.when(even)
    def _():
        own_p2.wait()
        wait_for(out_p, 63, psem.at[0])
        wait_for(out_p, 63, psem.at[3])
        wait_for(out_p, N - 1, psem.at[2])

    @pl.when(jnp.logical_not(even))
    def _():
        wait_for(out_p, 64, psem.at[0])
        wait_for(out_p, 64, psem.at[3])


def relocate_and_factor(adjusted_of, result_of, adjusted, base, sketch):
    smem = pl.BlockSpec(memory_space=pltpu.SMEM)
    anywhere = pl.BlockSpec(memory_space=pl.ANY)
    parts = len(CHUNKS)
    return pl.pallas_call(
        kernel,
        out_shape=(jax.ShapeDtypeStruct((32, 112, K), BF), jax.ShapeDtypeStruct((1024, K), BF)),
        in_specs=[smem, smem, anywhere, anywhere, pl.BlockSpec(memory_space=pltpu.VMEM)],
        out_specs=(anywhere, anywhere),
        scratch_shapes=[pltpu.VMEM((2 * N, rows, 256), BF) for _, rows in CHUNKS]
        + [pltpu.VMEM((N, rows, 256), BF) for _, rows in CHUNKS]
        + [
            pltpu.VMEM((32, 112, 1024), BF),
            pltpu.VMEM((224, 16, 1024), BF),
            pltpu.VMEM((K, ROWS), F32),
            pltpu.VMEM((K, 1024), F32),
            pltpu.VMEM((K, K), F32),
            pltpu.VMEM((K, K), F32),
            pltpu.VMEM((2, 10, 8, K), F32),
            pltpu.VMEM((112, 2, 16, K), BF),
            pltpu.VMEM((1024, K), BF),
            pltpu.VMEM((N, 2, 16, K), BF),
            pltpu.VMEM((N, 2, 16, K), BF),
            pltpu.VMEM((N, 16, K), BF),
            pltpu.VMEM((N, 16, K), BF),
        ]
        + [pltpu.SemaphoreType.DMA((parts,))] * 6
        + [pltpu.SemaphoreType.DMA((7,)), pltpu.SemaphoreType.DMA((6,)), pltpu.SemaphoreType.DMA((6,))],
        compiler_params=pltpu.CompilerParams(has_side_effects=True, vmem_limit_bytes=47 * 2**20),
        name="relocate_and_factor",
    )(adjusted_of, result_of, adjusted.reshape(2, 32, 112, 1024), base.reshape(1, 32, 112, 1024), sketch)


def by_key(key, value):
    places = lax.broadcasted_iota(jnp.int32, (N, N), 0)
    return jnp.sum(jnp.where(places == key[None, :], value[None, :], 0), axis=1, dtype=jnp.int32)


def shards(base_tiles, adjusted_tiles, sketch, base_place, adjusted_place, owner_map):
    adjusted_of = by_key(base_place, adjusted_place)
    result_of = by_key(owner_map, base_place)
    basis, projected = relocate_and_factor(adjusted_of, result_of, adjusted_tiles, base_tiles, sketch)
    scaled_basis = basis.reshape(ROWS, K).astype(F32) * math.sqrt(ROWS)
    projected = projected.astype(F32).reshape(8, K, K).transpose(1, 0, 2).reshape(K, 1024)
    return (scaled_basis[None], projected[None])


def solution(mesh):
    in_specs = (P(("grp", "ep"), None, None), P(("grp", "ep"), None, None), P(), P(), P(), P())
    out_specs = (P(("grp", "ep"), None, None), P(("grp", "ep"), None, None))
    return jax.shard_map(shards, mesh=mesh, in_specs=in_specs, out_specs=out_specs, check_vma=False)
```

```python
import math

import jax
import jax.numpy as jnp
from jax import lax
from jax.experimental import pallas as pl
from jax.experimental.pallas import tpu as pltpu
from jax.sharding import PartitionSpec as P

MESH = pl.DeviceIdType.MESH
N = 128
CHUNKS = ((0, 32), (32, 32), (64, 32), (96, 16))
F32 = jnp.float32
BF = jnp.bfloat16
NT = (((1,), (1,)), ((), ()))
NN = (((1,), (0,)), ((), ()))
TN = (((0,), (0,)), ((), ()))
K = 128
BLOCK = 32
C = 512
ROWS = 3584
HALF = ROWS // 2

def dot(a, b, dims):
    return lax.dot_general(a, b, dims, preferred_element_type=F32)

def split3(v):
    hi = v.astype(BF).astype(F32)
    rest = v - hi
    mid = rest.astype(BF).astype(F32)
    return hi, mid, rest - mid


def chol_inv(g_ref, w_ref, t_ref):
    sub = lax.broadcasted_iota(jnp.int32, (8, K), 0)
    a = g_ref[...]
    row = lax.broadcasted_iota(jnp.int32, (K, K), 0)
    col = lax.broadcasted_iota(jnp.int32, (K, K), 1)
    x = jnp.where(row == col, 1.0, 0.0).astype(F32)
    for b0 in range(0, K, BLOCK):
        panel = [a[i : i + 8] for i in range(0, BLOCK, 8)]
        side = [x[i : i + 8] for i in range(0, BLOCK, 8)]
        us = []
        ws = []
        for r0 in range(b0, b0 + BLOCK, 8):
            p = panel.pop(0)
            xp = side.pop(0)
            s = {}
            held = t_ref.at[r0 // 8 % 2]
            for k in range(8):
                held[k] = jnp.broadcast_to(p[:, r0 + k : r0 + k + 1], (8, K))
            held[8] = p
            held[9] = xp
            for i in range(8):
                for k in range(i + 1):
                    s[i, k] = jnp.broadcast_to(held[k, i : i + 1, :], (8, K))
            rows = [jnp.broadcast_to(held[8, i : i + 1, :], (8, K)) for i in range(8)]
            xrows = [jnp.broadcast_to(held[9, i : i + 1, :], (8, K)) for i in range(8)]
            below = [[jnp.broadcast_to(q[:, r0 + k : r0 + k + 1], (8, K)) for k in range(8)] for q in panel]
            u = jnp.zeros((8, K), F32)
            w = jnp.zeros((8, K), F32)
            for k in range(8):
                r = lax.rsqrt(s[k, k])
                uk = rows[k] * r
                wk = xrows[k] * r
                u = jnp.where(sub == k, uk, u)
                w = jnp.where(sub == k, wk, w)
                l = {i: s[i, k] * r for i in range(k + 1, 8)}
                for i in range(k + 1, 8):
                    for m in range(k + 1, i + 1):
                        s[i, m] = s[i, m] - l[i] * l[m]
                for i in range(k + 1, 8):
                    rows[i] = rows[i] - l[i] * uk
                    xrows[i] = xrows[i] - l[i] * wk
                for n, c in enumerate(below):
                    ck = c[k] * r
                    for m in range(k + 1, 8):
                        c[m] = c[m] - ck * l[m]
                    panel[n] = panel[n] - ck * uk
                    side[n] = side[n] - ck * wk
            w_ref[pl.ds(r0, 8), :] = w
            us.append(u)
            ws.append(w)
        if b0 < K - BLOCK:
            uh, um, ul = split3(jnp.concatenate(us, axis=0))
            wh, wm, wl = split3(jnp.concatenate(ws, axis=0))
            left = jnp.concatenate([uh, uh, um, uh, ul, um], axis=0).astype(BF)
            right = jnp.concatenate(
                [
                    jnp.concatenate([uh, um, uh, ul, uh, um], axis=0).astype(BF),
                    jnp.concatenate([wh, wm, wh, wl, wh, wm], axis=0).astype(BF),
                ],
                axis=1,
            )
            upd = dot(left, right, TN)
            a = a[BLOCK:] - upd[b0 + BLOCK :, :K]
            x = x[BLOCK:] - upd[b0 + BLOCK :, K:]


def wide_left(v):
    hi = v.astype(BF)
    return jnp.concatenate([hi, hi, (v - hi.astype(F32)).astype(BF)], axis=1)


def wide_right(v):
    hi = v.astype(BF)
    return jnp.concatenate([hi, (v - hi.astype(F32)).astype(BF), hi], axis=0)


def gram(v):
    hi, mid, low = (part.astype(BF) for part in split3(v))
    first = dot(hi, jnp.concatenate([hi, mid, low], axis=0), NT)
    cross = first[:, K : 2 * K] + first[:, 2 * K :]
    return first[:, :K] + dot(mid, mid, NT) + cross + cross.T


def peer(o):
    x = lax.axis_index("grp")
    e = lax.axis_index("ep")
    o = lax.rem(o * 101, 128)
    sign = 1 - 2 * lax.rem(e, 2)
    tx = lax.rem(x + 4 + sign * lax.div(o, 32), 4)
    tz = lax.rem(lax.div(e, 8) + 4 + sign * lax.rem(lax.div(o, 8), 4), 4)
    ty = lax.rem(lax.rem(lax.div(e, 2), 4) + 4 + sign * lax.rem(lax.div(o, 2), 4), 4)
    return tx, tz * 8 + ty * 2 + lax.rem(e + o, 2)


def whole(device):
    return None


def push(src, dst, send_sem, recv_sem, when=whole):
    def one(o, car):
        tx, te = peer(o)
        t = tx * 32 + te

        def start():
            pltpu.make_async_remote_copy(
                src(t), dst(t), send_sem, recv_sem, device_id=(tx, te), device_id_type=MESH
            ).start()

        if when is whole:
            start()
        else:
            pl.when(when(t))(start)
        return car

    lax.fori_loop(1, N, one, 0, unroll=3)


def wait_for(ref, count, sem):
    part = ref.at[pl.ds(0, count)]
    pltpu.make_async_copy(part, part, sem).wait()


def tile(i, chunk):
    first, rows = chunk
    return i // 4, pl.ds(first, rows), pl.ds(pl.multiple_of((i % 4) * 256, 256), 256)


def entry(i):
    return lax.rem(i * 37, N)


def basis_rows(ref, n):
    return ref.at[pl.ds(lax.rem(n, 16) * 2, 2), pl.ds(pl.multiple_of(lax.div(n, 16) * 16, 16), 16)]


def projected_rows(ref, i):
    return ref.at[pl.ds(pl.multiple_of((i // 2) * 16, 16), 16)]


def projected_tile(ref, i):
    unit = lax.div(i, 2)
    high = pl.ds(pl.multiple_of(lax.rem(unit, 8) * 16, 16), 16)
    return ref.at[high, pl.ds(pl.multiple_of(lax.div(unit, 8) * K, K), K)]


def kernel(adjusted_of, result_of, adjusted, base, sketch, basis_out, projected_out, *scratch):
    parts = len(CHUNKS)
    gots = scratch[:parts]
    outs = scratch[parts : 2 * parts]
    win, d, yt, zt, g, w, spread, basis, projected, got_q, out_q, got_p, out_p = scratch[2 * parts : 2 * parts + 13]
    ssem, rsem, s2sem, r2sem, lsem, l2sem, base_sem, qsem, psem = scratch[2 * parts + 13 :]
    me = lax.axis_index("grp") * 32 + lax.axis_index("ep")
    mine = pl.ds(2 * me, 2)

    base_copies = [
        pltpu.make_async_copy(base.at[0, :, pl.ds(16 * c, 16)], d.at[pl.ds(32 * c, 32)], base_sem.at[c]) for c in range(7)
    ]
    for copy in base_copies:
        copy.start()

    def stored(i, k):
        block, high, wide = tile(i, CHUNKS[k])
        return adjusted.at[:, block, high, wide]

    def landed(k):
        block, high, wide = tile(me, CHUNKS[k])
        return win.at[block, high, wide]

    def own(k):
        return pltpu.make_async_copy(stored(me, k), gots[k].at[mine], lsem.at[k])

    def own2(k):
        return pltpu.make_async_copy(outs[k].at[me], landed(k), l2sem.at[k])

    for k in range(parts):
        own(k).start()
        push(lambda t, k=k: stored(t, k), lambda t, k=k: gots[k].at[mine], ssem.at[k], rsem.at[k])
    st = sketch[...].astype(F32).T.astype(BF)
    for k in range(parts):
        own(k).wait()
        wait_for(gots[k], 2 * (N - 1), rsem.at[k])

        def pick(b, car, k=k):
            outs[k][b] = gots[k][adjusted_of[b]]
            return car

        lax.fori_loop(0, N, pick, 0, unroll=4)
        own2(k).start()
        push(lambda t, k=k: outs[k].at[t], lambda t, k=k: landed(k), s2sem.at[k], r2sem.at[k])

    for copy in base_copies:
        copy.wait()
    g[...] = jnp.zeros_like(g)

    def first(c, car):
        rows = pl.ds(pl.multiple_of(c * 16, 16), 16)
        held = pl.ds(pl.multiple_of(c * 32, 32), 32)
        here = pl.ds(pl.multiple_of(c * C, C), C)
        dc = (win[:, rows, :].astype(F32) - d[held].astype(F32)).astype(BF)
        d[held] = dc
        dc = dc.reshape(C, 1024)
        y = dot(st, dc, NT)
        yt[:, here] = y
        g[...] += gram(y)
        return car

    for k in range(parts):
        own2(k).wait()
        wait_for(outs[k], N - 1, r2sem.at[k])
        low, rows = CHUNKS[k]
        lax.fori_loop(low // 16, (low + rows) // 16, first, 0)

    halves = (pl.ds(0, HALF), pl.ds(HALF, HALF))

    def delta(n):
        return d[112 * n : 112 * (n + 1)].reshape(HALF, 1024)

    def step(t, car):
        chol_inv(g, w, spread)
        left = wide_left(w[...])

        @pl.when(t % 2 == 0)
        def _():
            total = jnp.zeros((K, 1024), F32)
            for n, h in enumerate(halves):
                q = dot(left, wide_right(yt[:, h]), NN)
                total = total + dot(q.astype(BF), delta(n), NN)
            zt[...] = total
            g[...] = gram(total)

        @pl.when(t % 2 == 1)
        def _():
            across = dot(left, wide_right(zt[...]), NN).astype(BF)
            total = jnp.zeros((K, K), F32)
            for n, h in enumerate(halves):
                y = dot(across, delta(n), NT)
                yt[:, h] = y
                total = total + gram(y)
            g[...] = total

        return car

    lax.fori_loop(0, 4, step, 0)
    chol_inv(g, w, spread)

    left = wide_left(w[...])
    for n, h in enumerate(halves):
        q = dot(left, wide_right(yt[:, h]), NN)
        basis[56 * n : 56 * (n + 1)] = q.T.astype(BF).reshape(56, 2, 16, K)
        yt[:, h] = q
    place = entry(me)
    relay = place < 112
    even = me % 2 == 0

    def both(condition, yes, no):
        pl.when(condition)(yes)
        pl.when(jnp.logical_not(condition))(no)

    own_q = pltpu.make_async_copy(basis.at[lax.rem(place, 112)], got_q.at[me], qsem.at[4])
    own_q2 = pltpu.make_async_copy(out_q.at[me], basis_rows(basis_out, place), qsem.at[5])
    own_p = pltpu.make_async_copy(projected_rows(projected, me), got_p.at[me], psem.at[4])
    own_p2 = pltpu.make_async_copy(out_p.at[me], projected_tile(projected_out, me), psem.at[5])

    push(lambda t: basis.at[entry(t)], lambda t: got_q.at[me], qsem.at[0], qsem.at[1], lambda t: entry(t) < 112)
    pl.when(relay)(own_q.start)

    total = jnp.zeros((K, 1024), F32)
    for n, h in enumerate(halves):
        total = total + dot(yt[:, h].astype(BF), delta(n), NN)
    for j in range(8):
        projected[K * j : K * (j + 1), :] = total[:, K * j : K * (j + 1)].astype(BF)
    push(lambda t: projected_rows(projected, t), lambda t: got_p.at[me], psem.at[0], psem.at[1], lambda t: t % 2 == 0)
    pl.when(even)(own_p.start)

    @pl.when(relay)
    def _():
        own_q.wait()
        wait_for(got_q, N - 1, qsem.at[1])

        def pick(b, car):
            out_q[b] = got_q[result_of[b]]
            return car

        lax.fori_loop(0, N, pick, 0, unroll=4)
        own_q2.start()
        push(lambda t: out_q.at[t], lambda t: basis_rows(basis_out, place), qsem.at[2], qsem.at[3])

    @pl.when(even)
    def _():
        own_p.wait()
        wait_for(got_p, N - 1, psem.at[1])

        def pick(b, car):
            out_p[b] = got_p[result_of[b]]
            return car

        lax.fori_loop(0, N, pick, 0, unroll=4)
        own_p2.start()
        push(lambda t: out_p.at[t], lambda t: projected_tile(projected_out, me), psem.at[2], psem.at[3])

    for k in range(parts):
        wait_for(gots[k], 2 * (N - 1), ssem.at[k])
        wait_for(outs[k], N - 1, s2sem.at[k])

    @pl.when(relay)
    def _():
        own_q2.wait()
        wait_for(out_q, 111, qsem.at[0])
        wait_for(out_q, 111, qsem.at[3])
        wait_for(out_q, N - 1, qsem.at[2])

    @pl.when(jnp.logical_not(relay))
    def _():
        wait_for(out_q, 112, qsem.at[0])
        wait_for(out_q, 112, qsem.at[3])

    @pl.when(even)
    def _():
        own_p2.wait()
        wait_for(out_p, 63, psem.at[0])
        wait_for(out_p, 63, psem.at[3])
        wait_for(out_p, N - 1, psem.at[2])

    @pl.when(jnp.logical_not(even))
    def _():
        wait_for(out_p, 64, psem.at[0])
        wait_for(out_p, 64, psem.at[3])


def relocate_and_factor(adjusted_of, result_of, adjusted, base, sketch):
    smem = pl.BlockSpec(memory_space=pltpu.SMEM)
    anywhere = pl.BlockSpec(memory_space=pl.ANY)
    parts = len(CHUNKS)
    return pl.pallas_call(
        kernel,
        out_shape=(jax.ShapeDtypeStruct((32, 112, K), BF), jax.ShapeDtypeStruct((K, 1024), BF)),
        in_specs=[smem, smem, anywhere, anywhere, pl.BlockSpec(memory_space=pltpu.VMEM)],
        out_specs=(anywhere, anywhere),
        scratch_shapes=[pltpu.VMEM((2 * N, rows, 256), BF) for _, rows in CHUNKS]
        + [pltpu.VMEM((N, rows, 256), BF) for _, rows in CHUNKS]
        + [
            pltpu.VMEM((32, 112, 1024), BF),
            pltpu.VMEM((224, 16, 1024), BF),
            pltpu.VMEM((K, ROWS), F32),
            pltpu.VMEM((K, 1024), F32),
            pltpu.VMEM((K, K), F32),
            pltpu.VMEM((K, K), F32),
            pltpu.VMEM((2, 10, 8, K), F32),
            pltpu.VMEM((112, 2, 16, K), BF),
            pltpu.VMEM((1024, K), BF),
            pltpu.VMEM((N, 2, 16, K), BF),
            pltpu.VMEM((N, 2, 16, K), BF),
            pltpu.VMEM((N, 16, K), BF),
            pltpu.VMEM((N, 16, K), BF),
        ]
        + [pltpu.SemaphoreType.DMA((parts,))] * 6
        + [pltpu.SemaphoreType.DMA((7,)), pltpu.SemaphoreType.DMA((6,)), pltpu.SemaphoreType.DMA((6,))],
        compiler_params=pltpu.CompilerParams(has_side_effects=True, vmem_limit_bytes=47 * 2**20),
        name="relocate_and_factor",
    )(adjusted_of, result_of, adjusted.reshape(2, 32, 112, 1024), base.reshape(1, 32, 112, 1024), sketch)


def by_key(key, value):
    places = lax.broadcasted_iota(jnp.int32, (N, N), 0)
    return jnp.sum(jnp.where(places == key[None, :], value[None, :], 0), axis=1, dtype=jnp.int32)


def shards(base_tiles, adjusted_tiles, sketch, base_place, adjusted_place, owner_map):
    adjusted_of = by_key(base_place, adjusted_place)
    result_of = by_key(owner_map, base_place)
    basis, projected = relocate_and_factor(adjusted_of, result_of, adjusted_tiles, base_tiles, sketch)
    scaled_basis = basis.reshape(ROWS, K).astype(F32) * math.sqrt(ROWS)
    return (scaled_basis[None], projected.astype(F32)[None])


def solution(mesh):
    in_specs = (P(("grp", "ep"), None, None), P(("grp", "ep"), None, None), P(), P(), P(), P())
    out_specs = (P(("grp", "ep"), None, None), P(("grp", "ep"), None, None))
    return jax.shard_map(shards, mesh=mesh, in_specs=in_specs, out_specs=out_specs, check_vma=False)
```
